32 devices in a mesh: ctx: 8 (over z, y), tp: 4 (over x, core).
Axes of the slice: x: 2, y: 2, z: 4, core: 2. Of those that a mesh axis runs over, the one named last changes fastest.
Arguments:
- tokens: bfloat16 [4096, 6144], P(('ctx', 'tp')), may hold values from -18 to 18
- w_query: bfloat16 [6144, 3072], P(None, 'tp'), may hold values from -1 to 1
- key_matrix: bfloat16 [6144, 512], P(None, 'tp'), may hold values from -1 to 1
- value_matrix: bfloat16 [6144, 512], P(None, 'tp'), may hold values from -0.078125 to 0.078125
- w_out: bfloat16 [3072, 6144], P('tp'), may hold values from -0.109375 to 0.109375
- span_order: int32 [8, 2], replicated, may hold values from 0 to 15, as said below
Outputs:
- attended: bfloat16 [4096, 6144], P(('ctx', 'tp'))
The draws below stay inside these ranges and needn't reach their ends.
Inputs may be any that keep to these rules, and one draw needn't show every extreme that they name: `span_order`: row r is (p, 15 - p) with p a permutation of 0 to 7, so every span appears once.
All inputs are finite; a program needn't handle non-finite values.
Results may differ from the reference program's by a relative error of at most 0.014.
The reference program's roundings to bfloat16 on the way count: a program that leaves them out, or rounds other values in their place, can miss the bound.
Values may be sent and summed in bfloat16 or wider, within the bound.
A program may use at most 128 MiB of HBM per device.

```python
import math
import jax
import jax.numpy as jnp
from jax import lax

MODEL_WIDTH = 6144
QUERY_HEADS = 24
KEY_HEADS = 4
HEAD_SIZE = 128
SPAN_TOKENS = 256
QUERY_PER_KEY = 6
SEQUENCE_TOKENS = 4096
N_CTX = 8
N_TP = 4


def unrotated_query(key):
    return jax.random.normal(jax.random.fold_in(key, 11), (MODEL_WIDTH, QUERY_HEADS * HEAD_SIZE), jnp.float32) * (3.0 / math.sqrt(MODEL_WIDTH))


def draw_w_query(key, part):
    return jnp.clip(unrotated_query(key), -1.0, 1.0).astype(jnp.bfloat16)


def draw_key_matrix(key, part):
    random_noise = jax.random.normal(jax.random.fold_in(key, 23), (MODEL_WIDTH, KEY_HEADS * HEAD_SIZE), jnp.float32) / math.sqrt(MODEL_WIDTH)
    mixed = random_noise
    return jnp.clip(mixed, -1.0, 1.0).astype(jnp.bfloat16)


def draw_tokens(key, part):
    normal_part = jnp.clip(jax.random.normal(jax.random.fold_in(key, 3), (SEQUENCE_TOKENS, MODEL_WIDTH), jnp.float32), -6.0, 6.0)
    result = normal_part
    return result.astype(jnp.bfloat16)


def draw_span_order(key, part):
    shuffled = jax.random.permutation(jax.random.fold_in(key, 7), N_CTX).astype(jnp.int32)
    return jnp.stack([shuffled, 2 * N_CTX - 1 - shuffled], axis=1).astype(jnp.int32)


def block_levels(stream_key, extent, pieces, low, largest):
    factor_of, own = 1.0, jax.random.fold_in(stream_key, 6)
    for position, shards_of in pieces:
        draws = jnp.exp(jax.random.uniform(jax.random.fold_in(own, position), (shards_of,), jnp.float32, low / len(pieces), largest / len(pieces)))
        factor_of = factor_of * jnp.repeat(draws, extent[position] // shards_of).reshape([-1 if axis == position else 1 for axis in range(len(extent))])
    return factor_of


def bell_draw(stream_key, dims, spread, most, split=(), kind=jnp.bfloat16):
    factor_of = block_levels(stream_key, dims, split, -0.22, 0.18) if split else 1.0
    values = jax.random.normal(stream_key, dims, jnp.float32) * spread * factor_of
    return jnp.minimum(jnp.maximum(values, -most), most).astype(kind)


def setup_inputs(seed: int = 0) -> dict:
    arg_keys = jax.random.split(jax.random.key(seed), 7)
    return {
        "tokens": draw_tokens(jax.random.fold_in(arg_keys[6], 71), 0),
        "w_query": draw_w_query(jax.random.fold_in(arg_keys[6], 71), 0),
        "key_matrix": draw_key_matrix(jax.random.fold_in(arg_keys[6], 71), 0),
        "value_matrix": bell_draw(arg_keys[3], (MODEL_WIDTH, KEY_HEADS * HEAD_SIZE), MODEL_WIDTH ** -0.5, 0.078125, ((1, 4),)),
        "w_out": bell_draw(arg_keys[4], (QUERY_HEADS * HEAD_SIZE, MODEL_WIDTH), (QUERY_HEADS * HEAD_SIZE) ** -0.5, 0.109375, ((0, 4),)),
        "span_order": draw_span_order(jax.random.fold_in(arg_keys[6], 71), 0),
    }


ROPE_BASE = 1000000.0

def rotary_embed(values, token_positions):
    half = values.shape[-1] // 2
    freq = ROPE_BASE ** (-(jnp.arange(half, dtype=jnp.float32) * 2.0) / values.shape[-1])
    angle = token_positions[:, None] * freq[None, :]
    cosine = jnp.cos(angle)[:, None, :]
    sine = jnp.sin(angle)[:, None, :]
    first = values[..., :half]
    second = values[..., half:]
    return jnp.concatenate([first * cosine - second * sine, second * cosine + first * sine], axis=-1)

def reference(tokens, w_query, key_matrix, value_matrix, w_out, span_order):
    flat = span_order.reshape(-1).astype(jnp.int32)
    rows = jnp.arange(SEQUENCE_TOKENS, dtype=jnp.int32)
    token_positions = (flat[rows // SPAN_TOKENS] * SPAN_TOKENS + rows % SPAN_TOKENS).astype(jnp.float32)
    query_rows = rotary_embed(jnp.dot(tokens, w_query, preferred_element_type=jnp.float32).reshape(SEQUENCE_TOKENS, QUERY_HEADS, HEAD_SIZE), token_positions).astype(jnp.bfloat16)
    key = rotary_embed(jnp.dot(tokens, key_matrix, preferred_element_type=jnp.float32).reshape(SEQUENCE_TOKENS, KEY_HEADS, HEAD_SIZE), token_positions).astype(jnp.bfloat16)
    value_rows = jnp.dot(tokens, value_matrix, preferred_element_type=jnp.float32).astype(jnp.bfloat16).reshape(SEQUENCE_TOKENS, KEY_HEADS, HEAD_SIZE)
    query_grouped = query_rows.reshape(N_CTX, 2 * SPAN_TOKENS, KEY_HEADS, QUERY_PER_KEY, HEAD_SIZE).transpose(2, 1, 0, 3, 4)
    query_grouped = query_grouped.transpose(0, 2, 1, 3, 4)
    block_pos = token_positions.reshape(N_CTX, 2 * SPAN_TOKENS)
    keys_t = key.transpose(1, 0, 2)
    values_t = value_rows.transpose(1, 0, 2)
    inv_scale = 1.0 / math.sqrt(HEAD_SIZE)

    def per_head(args):
        query_g, key_g, value_g = args
        key_f = key_g.astype(jnp.float32)
        value_f = value_g.astype(jnp.float32)

        def per_block(inner):
            query_b, pos_b = inner
            score = jnp.einsum('qgd,kd->gqk', query_b.astype(jnp.float32), key_f) * inv_scale
            keep = token_positions[None, None, :] <= pos_b[None, :, None]
            score = jnp.where(keep, score, -1e+30)
            top = lax.optimization_barrier(jnp.max(score, axis=-1, keepdims=True))
            weight = jnp.where(keep, jnp.exp(score - top), 0.0)
            total = lax.optimization_barrier(jnp.sum(weight, axis=-1))
            weight_b = weight.astype(jnp.bfloat16).astype(jnp.float32)
            mixed = jnp.einsum('gqk,kd->gqd', weight_b, value_f) / total[..., None]
            return mixed.astype(jnp.bfloat16).transpose(1, 0, 2)
        return lax.map(per_block, (query_g, block_pos))
    heads = lax.map(per_head, (query_grouped, keys_t, values_t))
    heads_out = heads.transpose(1, 2, 0, 3, 4).reshape(SEQUENCE_TOKENS, QUERY_HEADS * HEAD_SIZE)
    per = QUERY_HEADS * HEAD_SIZE // N_TP
    attended = jnp.zeros((SEQUENCE_TOKENS, MODEL_WIDTH), jnp.float32)
    for group_index in range(N_TP):
        partial_value = jnp.dot(heads_out[:, group_index * per:(group_index + 1) * per], w_out[group_index * per:(group_index + 1) * per], preferred_element_type=jnp.float32).astype(jnp.bfloat16)
        partial_value = lax.optimization_barrier(partial_value)
        attended = attended + partial_value.astype(jnp.float32)
    return attended.astype(jnp.bfloat16)
```

```python
import functools
import math

import jax
import jax.numpy as jnp
from jax import lax
from jax.experimental import pallas as pl
from jax.experimental.pallas import tpu as pltpu
from jax.sharding import PartitionSpec as P

ROPE_BASE = 1000000.0


def rotary_embed(values, token_positions):
    half = values.shape[-1] // 2
    freq = ROPE_BASE ** (-(jnp.arange(half, dtype=jnp.float32) * 2.0) / values.shape[-1])
    angle = token_positions[:, None] * freq[None, :]
    cosine = jnp.cos(angle)[:, None, :]
    sine = jnp.sin(angle)[:, None, :]
    first = values[..., :half]
    second = values[..., half:]
    return jnp.concatenate(
        [first * cosine - second * sine, second * cosine + first * sine], axis=-1
    )


LOG2_E = 1.4426950408889634


def attend_kernel(mine_ref, slots_ref, q_ref, kv_ref, o_ref, top_ref, total_ref, accum_ref):
    dim = kv_ref.shape[1] // 2
    span = q_ref.shape[0] // 2
    group = q_ref.shape[1] // dim
    parts = span // dim
    factor = LOG2_E / math.sqrt(dim)

    def tile(slot, half, first):
        start = pl.multiple_of(slot * span, span)
        key = kv_ref[pl.ds(start, span), :dim]
        value = kv_ref[pl.ds(start, span), dim:]
        if first:
            keep = lax.broadcasted_iota(jnp.int32, (span, span), 1) <= lax.broadcasted_iota(
                jnp.int32, (span, span), 0
            )
        for head in range(group):
            query = q_ref[half * span : (half + 1) * span, head * dim : (head + 1) * dim]
            score = lax.dot_general(
                query, key, (((1,), (1,)), ((), ())), preferred_element_type=jnp.float32
            )
            if first:
                score = jnp.where(keep, score, -1e30)
            top = jnp.broadcast_to(jnp.max(score, axis=1, keepdims=True), (span, dim))
            if not first:
                old = top_ref[head]
                top = jnp.maximum(old, top)
            weights = [
                jnp.exp2((score[:, part * dim : (part + 1) * dim] - top) * factor)
                for part in range(parts)
            ]
            total = functools.reduce(jnp.add, weights)
            weight = jnp.concatenate(weights, axis=1).astype(jnp.bfloat16)
            mixed = jnp.dot(weight, value, preferred_element_type=jnp.float32)
            if not first:
                scale = jnp.exp2((old - top) * factor)
                total = total_ref[head] * scale + total
                mixed = accum_ref[head] * scale + mixed
            top_ref[head] = top
            total_ref[head] = total
            accum_ref[head] = mixed

    for half in range(2):
        tile(2 * mine_ref[2] + half, half, True)

        def step(index, carry):
            tile(slots_ref[index], half, False)
            return carry

        lax.fori_loop(0, mine_ref[half], step, 0)
        for head in range(group):
            total = jnp.sum(total_ref[head], axis=1, keepdims=True)
            o_ref[half * span : (half + 1) * span, head * dim : (head + 1) * dim] = (
                accum_ref[head] / total
            ).astype(o_ref.dtype)


def attend(span_order, rank, query, kv):
    rows, columns = query.shape
    dim = kv.shape[1] // 2
    span = rows // 2
    group = columns // dim
    flat = span_order.reshape(-1)
    index = jnp.arange(flat.shape[0], dtype=jnp.int32)
    slots = jnp.sum(jnp.where(flat[None, :] == index[:, None], index[None, :], 0), axis=1)
    mine = lax.dynamic_slice(span_order, (rank, jnp.int32(0)), (1, 2)).reshape(2)
    mine = jnp.concatenate([mine, rank.astype(jnp.int32)[None]])
    return pl.pallas_call(
        attend_kernel,
        out_shape=jax.ShapeDtypeStruct((rows, columns), jnp.bfloat16),
        in_specs=[pl.BlockSpec(memory_space=pltpu.SMEM)] * 2
        + [pl.BlockSpec(memory_space=pltpu.VMEM)] * 2,
        out_specs=pl.BlockSpec(memory_space=pltpu.VMEM),
        scratch_shapes=[pltpu.VMEM((group, span, dim), jnp.float32)] * 3,
        compiler_params=pltpu.CompilerParams(vmem_limit_bytes=40 * 2**20),
        name="attend",
    )(mine, slots, query, kv)


def body(tokens, w_query, key_matrix, value_matrix, w_out, span_order):
    rank = lax.axis_index("ctx")
    head_dim = key_matrix.shape[1]
    qcols = w_query.shape[1]
    group = qcols // head_dim
    piece = lax.all_gather(tokens, "tp", axis=0, tiled=True)
    block_rows = piece.shape[0]
    span = block_rows // 2
    mine = lax.dynamic_slice(span_order, (rank, jnp.int32(0)), (1, 2)).reshape(2)
    own_pos = (
        (mine[:, None] * span + jnp.arange(span, dtype=jnp.int32)[None, :])
        .reshape(-1)
        .astype(jnp.float32)
    )
    key = jnp.dot(piece, key_matrix, preferred_element_type=jnp.float32)
    value = jnp.dot(piece, value_matrix, preferred_element_type=jnp.float32).astype(jnp.bfloat16)
    key = (
        rotary_embed(key.reshape(block_rows, 1, head_dim), own_pos)
        .reshape(block_rows, head_dim)
        .astype(jnp.bfloat16)
    )
    kv = lax.all_gather(jnp.concatenate([key, value], axis=1), "ctx", axis=0, tiled=True)
    query = jnp.dot(piece, w_query, preferred_element_type=jnp.float32)
    query = (
        rotary_embed(query.reshape(block_rows, group, head_dim), own_pos)
        .astype(jnp.bfloat16)
        .reshape(block_rows, qcols)
    )
    heads_out = attend(span_order, rank, query, kv)
    return lax.psum_scatter(
        jnp.dot(heads_out, w_out, preferred_element_type=jnp.float32).astype(jnp.bfloat16),
        "tp",
        scatter_dimension=0,
        tiled=True,
    )


def solution(mesh):
    return jax.shard_map(
        body,
        mesh=mesh,
        in_specs=(
            P(("ctx", "tp"), None),
            P(None, "tp"),
            P(None, "tp"),
            P(None, "tp"),
            P("tp", None),
            P(),
        ),
        out_specs=P(("ctx", "tp"), None),
        check_vma=False,
    )
```

```python
import functools
import math

import jax
import jax.numpy as jnp
from jax import lax
from jax.experimental import pallas as pl
from jax.experimental.pallas import tpu as pltpu
from jax.sharding import PartitionSpec as P

ROPE_BASE = 1000000.0


LOG2_E = 1.4426950408889634


def attend_kernel(mine_ref, slots_ref, q_ref, kv_ref, o_ref, top_ref, total_ref, accum_ref):
    dim = kv_ref.shape[1] // 2
    span = q_ref.shape[0] // 2
    group = q_ref.shape[1] // dim
    parts = span // dim
    factor = LOG2_E / math.sqrt(dim)

    def tile(slot, half, first):
        start = pl.multiple_of(slot * span, span)
        key = kv_ref[pl.ds(start, span), :dim]
        value = kv_ref[pl.ds(start, span), dim:]
        if first:
            keep = lax.broadcasted_iota(jnp.int32, (span, span), 1) <= lax.broadcasted_iota(
                jnp.int32, (span, span), 0
            )
        for head in range(group):
            query = q_ref[half * span : (half + 1) * span, head * dim : (head + 1) * dim]
            score = lax.dot_general(
                query, key, (((1,), (1,)), ((), ())), preferred_element_type=jnp.float32
            )
            if first:
                score = jnp.where(keep, score, -1e30)
            top = jnp.broadcast_to(jnp.max(score, axis=1, keepdims=True), (span, dim))
            if not first:
                old = top_ref[head]
                top = jnp.maximum(old, top)
            weights = [
                jnp.exp2((score[:, part * dim : (part + 1) * dim] - top) * factor)
                for part in range(parts)
            ]
            total = functools.reduce(jnp.add, weights)
            weight = jnp.concatenate(weights, axis=1).astype(jnp.bfloat16)
            mixed = jnp.dot(weight, value, preferred_element_type=jnp.float32)
            if not first:
                scale = jnp.exp2((old - top) * factor)
                total = total_ref[head] * scale + total
                mixed = accum_ref[head] * scale + mixed
            top_ref[head] = top
            total_ref[head] = total
            accum_ref[head] = mixed

    for half in range(2):
        tile(2 * mine_ref[2] + half, half, True)

        def step(index, carry):
            tile(slots_ref[index], half, False)
            return carry

        lax.fori_loop(0, mine_ref[half], step, 0)
        for head in range(group):
            total = jnp.sum(total_ref[head], axis=1, keepdims=True)
            o_ref[half * span : (half + 1) * span, head * dim : (head + 1) * dim] = (
                accum_ref[head] / total
            ).astype(o_ref.dtype)


def attend(span_order, rank, query, kv):
    rows, columns = query.shape
    dim = kv.shape[1] // 2
    span = rows // 2
    group = columns // dim
    flat = span_order.reshape(-1)
    index = jnp.arange(flat.shape[0], dtype=jnp.int32)
    slots = jnp.sum(jnp.where(flat[None, :] == index[:, None], index[None, :], 0), axis=1)
    mine = lax.dynamic_slice(span_order, (rank, jnp.int32(0)), (1, 2)).reshape(2)
    mine = jnp.concatenate([mine, rank.astype(jnp.int32)[None]])
    return pl.pallas_call(
        attend_kernel,
        out_shape=jax.ShapeDtypeStruct((rows, columns), jnp.bfloat16),
        in_specs=[pl.BlockSpec(memory_space=pltpu.SMEM)] * 2
        + [pl.BlockSpec(memory_space=pltpu.VMEM)] * 2,
        out_specs=pl.BlockSpec(memory_space=pltpu.VMEM),
        scratch_shapes=[pltpu.VMEM((group, span, dim), jnp.float32)] * 3,
        compiler_params=pltpu.CompilerParams(vmem_limit_bytes=40 * 2**20),
        name="attend",
    )(mine, slots, query, kv)


MESH = pl.DeviceIdType.MESH
PIECES = 4
CHUNKS = 8


def greet(devices):
    barrier = pltpu.get_barrier_semaphore()
    for device in devices:
        pl.semaphore_signal(barrier, inc=1, device_id=device, device_id_type=MESH)
    pl.semaphore_wait(barrier, len(devices))


def pair_places():
    place = lax.axis_index("tp")
    chip = place // 2
    core = place % 2
    return chip, core, {"tp": chip * 2 + 1 - core}, {"tp": (1 - chip) * 2 + core}


def project_kernel(
    columns_apart,
    ranks,
    tokens_ref,
    w_query_ref,
    key_matrix_ref,
    value_matrix_ref,
    cosine_ref,
    sine_ref,
    query_ref,
    kv_ref,
    weights,
    near,
    far,
    kv_near,
    kv_far,
    weight_sems,
    local_sems,
    near_sems,
    far_sems,
    swap_sems,
    column_sems,
    row_sems,
):
    chip, core, partner, across = pair_places()
    rank = lax.axis_index("ctx")
    tall = ranks // columns_apart
    wide = columns_apart
    row = rank // wide
    column = rank % wide
    count, piece = far.shape[0], far.shape[2]
    rows, width = tokens_ref.shape
    dim = key_matrix_ref.shape[1]
    blocks = weights.shape[0] - 1
    block = weights.shape[2]

    def along_rows(step):
        return {"ctx": lax.rem(row + step, tall) * wide + column}

    def along_columns(step):
        return {"ctx": row * wide + lax.rem(column + step, wide)}

    greet(
        [partner, across]
        + [along_rows(step) for step in range(1, tall)]
        + [along_columns(step) for step in range(1, wide)]
    )

    def remote(source, target, sems, index, device):
        return pltpu.make_async_remote_copy(
            src_ref=source,
            dst_ref=target,
            send_sem=sems.at[(0,) + index],
            recv_sem=sems.at[(1,) + index],
            device_id=device,
            device_id_type=MESH,
        )

    far_copies = []
    for part in range(count):
        copy = remote(
            tokens_ref.at[pl.ds(part * piece, piece)],
            far.at[part, core],
            far_sems,
            (part,),
            across,
        )
        copy.start()
        far_copies.append(copy)
    near_copy = remote(tokens_ref, near.at[core], near_sems, (), partner)
    near_copy.start()
    own_copy = pltpu.make_async_copy(tokens_ref, near.at[core], local_sems.at[0])
    own_copy.start()
    loads = [
        pltpu.make_async_copy(
            key_matrix_ref, weights.at[blocks, :, pl.ds(0, dim)], weight_sems.at[blocks]
        ),
        pltpu.make_async_copy(
            value_matrix_ref, weights.at[blocks, :, pl.ds(dim, dim)], weight_sems.at[blocks + 1]
        ),
    ]
    for index in range(blocks):
        loads.append(
            pltpu.make_async_copy(
                w_query_ref.at[:, pl.ds(index * block, block)],
                weights.at[index],
                weight_sems.at[index],
            )
        )
    for load in loads:
        load.start()

    def place(part, source):
        if part == 0:
            return kv_ref.at[source, chip]
        return kv_ref.at[source, 1 - chip, :, pl.ds((part - 1) * piece, piece)]

    def tables(part):
        if part == 0:
            return cosine_ref[chip], sine_ref[chip]
        span = slice((part - 1) * piece, part * piece)
        return cosine_ref[1 - chip, :, span], sine_ref[1 - chip, :, span]

    def flat(values):
        return values.reshape(values.shape[0] * values.shape[1], values.shape[2])

    def rotate(values, cosine, sine):
        return values * cosine + pltpu.roll(values, dim // 2, 1) * sine

    waits = []

    def share(part, staged):
        local = pltpu.make_async_copy(staged, place(part, rank), local_sems.at[1 + part])
        local.start()
        waits.append(local.wait)
        row_copies = []
        for step in range(1, tall):
            copy = remote(
                staged, place(part, rank), row_sems, (part, step - 1), along_rows(step)
            )
            copy.start()
            row_copies.append(copy)
            waits.append(copy.wait_send)
        for step in range(1, wide):
            copy = remote(
                staged, place(part, rank), column_sems, (part, 0, step - 1), along_columns(step)
            )
            copy.start()
            waits.append(copy.wait_send)

    def pass_on(part):
        for step in range(1, tall):
            source = lax.rem(row + tall - step, tall) * wide + column
            remote(
                place(part, source),
                place(part, source),
                row_sems,
                (part, step - 1),
                along_rows(step),
            ).wait_recv()
            for side in range(1, wide):
                copy = remote(
                    place(part, source),
                    place(part, source),
                    column_sems,
                    (part, step, side - 1),
                    along_columns(side),
                )
                copy.start()
                waits.append(copy.wait_send)

    def work(part, held, staged):
        cosine, sine = tables(part)
        cosine, sine = flat(cosine), flat(sine)
        both = jnp.dot(flat(held[...]), weights[blocks], preferred_element_type=jnp.float32)
        key = rotate(both[:, :dim], cosine, sine)
        kept = jnp.concatenate([key, both[:, dim:]], axis=1).astype(jnp.bfloat16)
        staged[...] = kept.reshape(staged.shape)
        share(part, staged)
        if part == 0:
            for load in loads[2:]:
                load.wait()

        def one_block(index, carry):
            found = jnp.dot(flat(held[...]), weights[index], preferred_element_type=jnp.float32)
            for head in range(block // dim):
                turned = rotate(found[:, head * dim : (head + 1) * dim], cosine, sine)
                turned = turned.astype(jnp.bfloat16).reshape(2, -1, dim)
                lanes = pl.ds(pl.multiple_of(index * block + head * dim, dim), dim)
                if part == 0:
                    query_ref[chip, :, :, lanes] = turned
                else:
                    query_ref[1 - chip, :, (part - 1) * piece : part * piece, lanes] = turned
            return carry

        lax.fori_loop(0, blocks, one_block, 0)

    own_copy.wait()
    near_copy.wait()
    for load in loads[:2]:
        load.wait()
    work(0, near, kv_near)
    for part in range(count):
        far_copies[part].wait_recv()
        swap = remote(far.at[part, core], far.at[part, core], swap_sems, (part,), partner)
        swap.start()
        pass_on(part)
        swap.wait()
        work(part + 1, far.at[part], kv_far.at[part])
    pass_on(count)
    for copy in far_copies:
        copy.wait_send()
    for part in range(count + 1):
        for step in range(tall):
            for side in range(1, wide):
                source = lax.rem(row + tall - step, tall) * wide + lax.rem(
                    column + wide - side, wide
                )
                remote(
                    place(part, source),
                    place(part, source),
                    column_sems,
                    (part, step, side - 1),
                    along_columns(side),
                ).wait_recv()
    for wait in waits:
        wait()


def project(tokens, w_query, key_matrix, value_matrix, cosine, sine):
    ranks = lax.axis_size("ctx")
    wide = 4 if ranks % 16 == 0 else 2
    rows, width = tokens.shape
    dim = key_matrix.shape[1]
    columns = w_query.shape[1]
    block = 2 * dim
    blocks = columns // block
    piece = rows // PIECES
    dma = pltpu.SemaphoreType.DMA
    bf16 = jnp.bfloat16
    return pl.pallas_call(
        functools.partial(project_kernel, wide, ranks),
        out_shape=(
            jax.ShapeDtypeStruct((2, 2, rows, columns), bf16),
            jax.ShapeDtypeStruct((ranks, 2, 2, rows, 2 * dim), bf16),
        ),
        in_specs=[pl.BlockSpec(memory_space=pl.ANY)] * 4
        + [pl.BlockSpec(memory_space=pltpu.VMEM)] * 2,
        out_specs=(pl.BlockSpec(memory_space=pltpu.VMEM), pl.BlockSpec(memory_space=pl.ANY)),
        scratch_shapes=[
            pltpu.VMEM((blocks + 1, width, block), bf16),
            pltpu.VMEM((2, rows, width), bf16),
            pltpu.VMEM((PIECES, 2, piece, width), bf16),
            pltpu.VMEM((2, rows, block), bf16),
            pltpu.VMEM((PIECES, 2, piece, block), bf16),
            dma((blocks + 2,)),
            dma((PIECES + 2,)),
            dma((2,)),
            dma((2, PIECES)),
            dma((2, PIECES)),
            dma((2, PIECES + 1, ranks // wide, wide - 1)),
            dma((2, PIECES + 1, ranks // wide - 1)),
        ],
        compiler_params=pltpu.CompilerParams(
            collective_id=0, has_side_effects=True, vmem_limit_bytes=48 * 2**20
        ),
        name="project",
    )(tokens, w_query, key_matrix, value_matrix, cosine, sine)


def combine_kernel(
    heads_ref,
    w_ref,
    out_ref,
    weights,
    cross_part,
    pair_in,
    cross_out,
    cross_in,
    own_part,
    own_in,
    weight_sems,
    pair_sems,
    cross_sems,
    own_sems,
):
    chip, core, partner, across = pair_places()
    chunks, _, width = weights.shape
    rows = out_ref.shape[0]
    loads = [
        pltpu.make_async_copy(
            w_ref.at[:, pl.ds(index * width, width)], weights.at[index], weight_sems.at[index]
        )
        for index in range(chunks)
    ]
    for load in loads:
        load.start()
    greet([partner, across])

    def remote(source, target, sems, index, device):
        return pltpu.make_async_remote_copy(
            src_ref=source,
            dst_ref=target,
            send_sem=sems.at[0, index],
            recv_sem=sems.at[1, index],
            device_id=device,
            device_id_type=MESH,
        )

    def pair_copy(index):
        return remote(
            cross_part.at[index, 1 - core], pair_in.at[index], pair_sems, index, partner
        )

    def cross_copy(index):
        return remote(cross_out.at[index], cross_in.at[index], cross_sems, index, across)

    def own_copy(index):
        return remote(own_part.at[index, 1 - core], own_in.at[index], own_sems, index, partner)

    def partial(side, index):
        heads = heads_ref[side].reshape(2 * rows, heads_ref.shape[3])
        found = jnp.dot(heads, weights[index], preferred_element_type=jnp.float32)
        return found.astype(jnp.bfloat16).reshape(2, rows, width)

    def add_pair(index):
        pair_copy(index).wait_recv()
        cross_out[index] = (
            cross_part[index, core].astype(jnp.float32) + pair_in[index].astype(jnp.float32)
        ).astype(jnp.bfloat16)
        cross_copy(index).start()

    def first(index, carry):
        pltpu.make_async_copy(weights.at[index], weights.at[index], weight_sems.at[index]).wait()
        cross_part[index] = partial(1 - chip, index)
        pair_copy(index).start()

        @pl.when(index > 0)
        def _():
            add_pair(index - 1)

        return carry

    lax.fori_loop(0, chunks, first, 0)
    add_pair(chunks - 1)

    def second(index, carry):
        own_part[index] = partial(chip, index)
        own_copy(index).start()
        return carry

    lax.fori_loop(0, chunks, second, 0)

    def last(index, carry):
        own_copy(index).wait()
        pair_copy(index).wait_send()
        cross_copy(index).wait()
        total = own_part[index, core].astype(jnp.float32) + own_in[index].astype(jnp.float32)
        total = total + cross_in[index].astype(jnp.float32)
        out_ref[:, pl.ds(pl.multiple_of(index * width, width), width)] = total.astype(jnp.bfloat16)
        return carry

    lax.fori_loop(0, chunks, last, 0)


def combine(heads_out, w_out):
    depth, columns = w_out.shape
    rows = heads_out.shape[0] // 4
    width = columns // CHUNKS
    dma = pltpu.SemaphoreType.DMA
    bf16 = jnp.bfloat16
    single = pltpu.VMEM((CHUNKS, rows, width), bf16)
    double = pltpu.VMEM((CHUNKS, 2, rows, width), bf16)
    return pl.pallas_call(
        combine_kernel,
        out_shape=jax.ShapeDtypeStruct((rows, columns), bf16),
        in_specs=[pl.BlockSpec(memory_space=pltpu.VMEM), pl.BlockSpec(memory_space=pl.ANY)],
        out_specs=pl.BlockSpec(memory_space=pltpu.VMEM),
        scratch_shapes=[
            pltpu.VMEM((CHUNKS, depth, width), bf16),
            double,
            single,
            single,
            single,
            double,
            single,
            dma((CHUNKS,)),
            dma((2, CHUNKS)),
            dma((2, CHUNKS)),
            dma((2, CHUNKS)),
        ],
        compiler_params=pltpu.CompilerParams(
            collective_id=1, has_side_effects=True, vmem_limit_bytes=48 * 2**20
        ),
        name="combine",
    )(heads_out.reshape(2, 2, rows, depth), w_out)


def body(tokens, w_query, key_matrix, value_matrix, w_out, span_order):
    rank = lax.axis_index("ctx")
    dim = key_matrix.shape[1]
    half = dim // 2
    rows = tokens.shape[0]
    span = 2 * rows
    mine = lax.dynamic_slice(span_order, (rank, jnp.int32(0)), (1, 2)).reshape(2)
    own_pos = (
        (mine[:, None] * span + jnp.arange(span, dtype=jnp.int32)[None, :])
        .reshape(-1)
        .astype(jnp.float32)
    )
    freq = ROPE_BASE ** (-(jnp.arange(half, dtype=jnp.float32) * 2.0) / dim)
    angle = own_pos[:, None] * freq[None, :]
    cosine, sine = jnp.cos(angle), jnp.sin(angle)
    cosine = jnp.concatenate([cosine, cosine], axis=1).reshape(2, 2, rows, dim)
    sine = jnp.concatenate([-sine, sine], axis=1).reshape(2, 2, rows, dim)
    query, kv = project(tokens, w_query, key_matrix, value_matrix, cosine, sine)
    heads_out = attend(
        span_order, rank, query.reshape(4 * rows, -1), kv.reshape(-1, 2 * dim)
    )
    return combine(heads_out, w_out)


def solution(mesh):
    return jax.shard_map(
        body,
        mesh=mesh,
        in_specs=(
            P(("ctx", "tp"), None),
            P(None, "tp"),
            P(None, "tp"),
            P(None, "tp"),
            P("tp", None),
            P(),
        ),
        out_specs=P(("ctx", "tp"), None),
        check_vma=False,
    )
```

```python
import functools
import math

import jax
import jax.numpy as jnp
from jax import lax
from jax.experimental import pallas as pl
from jax.experimental.pallas import tpu as pltpu
from jax.sharding import PartitionSpec as P

ROPE_BASE = 1000000.0


LOG2_E = 1.4426950408889634


MESH = pl.DeviceIdType.MESH
PIECES = 4
STRIPS = 4
CHUNKS = 4


def greet(devices):
    barrier = pltpu.get_barrier_semaphore()
    for device in devices:
        pl.semaphore_signal(barrier, inc=1, device_id=device, device_id_type=MESH)
    pl.semaphore_wait(barrier, len(devices))


def pair_places():
    place = lax.axis_index("tp")
    chip = place // 2
    core = place % 2
    return chip, core, {"tp": chip * 2 + 1 - core}, {"tp": (1 - chip) * 2 + core}


def project_kernel(
    columns_apart,
    ranks,
    tokens_ref,
    w_query_ref,
    key_matrix_ref,
    value_matrix_ref,
    cosine_ref,
    sine_ref,
    query_ref,
    kv_ref,
    weights,
    near,
    far,
    kv_near,
    kv_far,
    weight_sems,
    local_sems,
    near_sems,
    far_sems,
    swap_sems,
    column_sems,
    row_sems,
):
    chip, core, partner, across = pair_places()
    rank = lax.axis_index("ctx")
    tall = ranks // columns_apart
    wide = columns_apart
    row = rank // wide
    column = rank % wide
    count, piece = far.shape[0], far.shape[2]
    rows, width = tokens_ref.shape
    dim = key_matrix_ref.shape[1]
    blocks = weights.shape[0] - 1
    block = weights.shape[2]

    def along_rows(step):
        return {"ctx": lax.rem(row + step, tall) * wide + column}

    def along_columns(step):
        return {"ctx": row * wide + lax.rem(column + step, wide)}

    greet(
        [partner, across]
        + [along_rows(step) for step in range(1, tall)]
        + [along_columns(step) for step in range(1, wide)]
    )

    def remote(source, target, sems, index, device):
        return pltpu.make_async_remote_copy(
            src_ref=source,
            dst_ref=target,
            send_sem=sems.at[(0,) + index],
            recv_sem=sems.at[(1,) + index],
            device_id=device,
            device_id_type=MESH,
        )

    far_copies = []
    for part in range(count):
        copy = remote(
            tokens_ref.at[pl.ds(part * piece, piece)],
            far.at[part, core],
            far_sems,
            (part,),
            across,
        )
        copy.start()
        far_copies.append(copy)
    near_copy = remote(tokens_ref, near.at[core], near_sems, (), partner)
    near_copy.start()
    own_copy = pltpu.make_async_copy(tokens_ref, near.at[core], local_sems.at[0])
    own_copy.start()
    loads = [
        pltpu.make_async_copy(
            key_matrix_ref, weights.at[blocks, :, pl.ds(0, dim)], weight_sems.at[blocks]
        ),
        pltpu.make_async_copy(
            value_matrix_ref, weights.at[blocks, :, pl.ds(dim, dim)], weight_sems.at[blocks + 1]
        ),
    ]
    for index in range(blocks):
        loads.append(
            pltpu.make_async_copy(
                w_query_ref.at[:, pl.ds(index * block, block)],
                weights.at[index],
                weight_sems.at[index],
            )
        )
    for load in loads:
        load.start()

    def place(part, source):
        if part == 0:
            return kv_ref.at[source, chip]
        return kv_ref.at[source, 1 - chip, :, pl.ds((part - 1) * piece, piece)]

    def tables(part):
        if part == 0:
            return cosine_ref[chip], sine_ref[chip]
        span = slice((part - 1) * piece, part * piece)
        return cosine_ref[1 - chip, :, span], sine_ref[1 - chip, :, span]

    def flat(values):
        return values.reshape(values.shape[0] * values.shape[1], values.shape[2])

    def rotate(values, cosine, sine):
        return values * cosine + pltpu.roll(values, dim // 2, 1) * sine

    waits = []

    def share(part, staged):
        local = pltpu.make_async_copy(staged, place(part, rank), local_sems.at[1 + part])
        local.start()
        waits.append(local.wait)
        row_copies = []
        for step in range(1, tall):
            copy = remote(
                staged, place(part, rank), row_sems, (part, step - 1), along_rows(step)
            )
            copy.start()
            row_copies.append(copy)
            waits.append(copy.wait_send)
        for step in range(1, wide):
            copy = remote(
                staged, place(part, rank), column_sems, (part, 0, step - 1), along_columns(step)
            )
            copy.start()
            waits.append(copy.wait_send)

    def pass_on(part):
        for step in range(1, tall):
            source = lax.rem(row + tall - step, tall) * wide + column
            remote(
                place(part, source),
                place(part, source),
                row_sems,
                (part, step - 1),
                along_rows(step),
            ).wait_recv()
            for side in range(1, wide):
                copy = remote(
                    place(part, source),
                    place(part, source),
                    column_sems,
                    (part, step, side - 1),
                    along_columns(side),
                )
                copy.start()
                waits.append(copy.wait_send)

    def work(part, held, staged):
        cosine, sine = tables(part)
        cosine, sine = flat(cosine), flat(sine)
        both = jnp.dot(flat(held[...]), weights[blocks], preferred_element_type=jnp.float32)
        key = rotate(both[:, :dim], cosine, sine)
        kept = jnp.concatenate([key, both[:, dim:]], axis=1).astype(jnp.bfloat16)
        staged[...] = kept.reshape(staged.shape)
        share(part, staged)
        if part == 0:
            for load in loads[2:]:
                load.wait()

        def one_block(index, carry):
            found = jnp.dot(flat(held[...]), weights[index], preferred_element_type=jnp.float32)
            for head in range(block // dim):
                turned = rotate(found[:, head * dim : (head + 1) * dim], cosine, sine)
                turned = turned.astype(jnp.bfloat16).reshape(2, -1, dim)
                lanes = pl.ds(pl.multiple_of(index * block + head * dim, dim), dim)
                if part == 0:
                    query_ref[chip, :, :, lanes] = turned
                else:
                    query_ref[1 - chip, :, (part - 1) * piece : part * piece, lanes] = turned
            return carry

        lax.fori_loop(0, blocks, one_block, 0)

    own_copy.wait()
    near_copy.wait()
    for load in loads[:2]:
        load.wait()
    work(0, near, kv_near)
    for part in range(count):
        far_copies[part].wait_recv()
        swap = remote(far.at[part, core], far.at[part, core], swap_sems, (part,), partner)
        swap.start()
        pass_on(part)
        swap.wait()
        work(part + 1, far.at[part], kv_far.at[part])
    pass_on(count)
    for copy in far_copies:
        copy.wait_send()
    for part in range(count + 1):
        for step in range(tall):
            for side in range(1, wide):
                source = lax.rem(row + tall - step, tall) * wide + lax.rem(
                    column + wide - side, wide
                )
                remote(
                    place(part, source),
                    place(part, source),
                    column_sems,
                    (part, step, side - 1),
                    along_columns(side),
                ).wait_recv()
    for wait in waits:
        wait()


def project(tokens, w_query, key_matrix, value_matrix, cosine, sine):
    ranks = lax.axis_size("ctx")
    wide = 4 if ranks % 16 == 0 else 2
    rows, width = tokens.shape
    dim = key_matrix.shape[1]
    columns = w_query.shape[1]
    block = 2 * dim
    blocks = columns // block
    piece = rows // PIECES
    dma = pltpu.SemaphoreType.DMA
    bf16 = jnp.bfloat16
    return pl.pallas_call(
        functools.partial(project_kernel, wide, ranks),
        out_shape=(
            jax.ShapeDtypeStruct((2, 2, rows, columns), bf16),
            jax.ShapeDtypeStruct((ranks, 2, 2, rows, 2 * dim), bf16),
        ),
        in_specs=[pl.BlockSpec(memory_space=pl.ANY)] * 4
        + [pl.BlockSpec(memory_space=pltpu.VMEM)] * 2,
        out_specs=(pl.BlockSpec(memory_space=pltpu.VMEM), pl.BlockSpec(memory_space=pl.ANY)),
        scratch_shapes=[
            pltpu.VMEM((blocks + 1, width, block), bf16),
            pltpu.VMEM((2, rows, width), bf16),
            pltpu.VMEM((PIECES, 2, piece, width), bf16),
            pltpu.VMEM((2, rows, block), bf16),
            pltpu.VMEM((PIECES, 2, piece, block), bf16),
            dma((blocks + 2,)),
            dma((PIECES + 2,)),
            dma((2,)),
            dma((2, PIECES)),
            dma((2, PIECES)),
            dma((2, PIECES + 1, ranks // wide, wide - 1)),
            dma((2, PIECES + 1, ranks // wide - 1)),
        ],
        compiler_params=pltpu.CompilerParams(
            collective_id=0, has_side_effects=True, vmem_limit_bytes=60 * 2**20
        ),
        name="project",
    )(tokens, w_query, key_matrix, value_matrix, cosine, sine)


def combine_kernel(
    ranks,
    spans_ref,
    query_ref,
    kv_hbm_ref,
    w_ref,
    out_ref,
    kv_ref,
    weights,
    queries,
    tops,
    totals,
    accums,
    heads_out,
    cross_part,
    pair_in,
    cross_out,
    cross_in,
    own_part,
    own_in,
    kv_sem,
    weight_sems,
    pair_sems,
    cross_sems,
    own_sems,
):
    chip, core, partner, across = pair_places()
    rank = lax.axis_index("ctx")
    chunks, _, width = weights.shape
    rows = query_ref.shape[2]
    span = 2 * rows
    dim = kv_ref.shape[1] // 2
    strip = heads_out.shape[0] // 2
    strips = rows // strip
    sets, stacked, _ = queries.shape
    group = stacked // (2 * strip)
    parts = span // dim
    factor = LOG2_E / math.sqrt(dim)

    kv_load = pltpu.make_async_copy(kv_hbm_ref, kv_ref, kv_sem)
    kv_load.start()
    loads = [
        pltpu.make_async_copy(
            w_ref.at[:, pl.ds(index * width, width)], weights.at[index], weight_sems.at[index]
        )
        for index in range(chunks)
    ]
    for load in loads:
        load.start()
    greet([partner, across])
    kv_load.wait()

    def remote(source, target, sems, index, device):
        return pltpu.make_async_remote_copy(
            src_ref=source,
            dst_ref=target,
            send_sem=sems.at[0, index],
            recv_sem=sems.at[1, index],
            device_id=device,
            device_id_type=MESH,
        )

    def pair_copy(index):
        return remote(
            cross_part.at[index, 1 - core], pair_in.at[index], pair_sems, index, partner
        )

    def cross_copy(index):
        return remote(cross_out.at[index], cross_in.at[index], cross_sems, index, across)

    def own_copy(index):
        return remote(own_part.at[index, 1 - core], own_in.at[index], own_sems, index, partner)

    def key_tile(slot):
        start = pl.multiple_of(slot * span, span)
        return kv_ref[pl.ds(start, span), :dim], kv_ref[pl.ds(start, span), dim:]

    def attend_strip(half, index):
        start = pl.multiple_of(index * strip, strip)
        for one in range(sets):
            for head in range(group):
                at = (one * group + head) * dim
                queries[one, head * 2 * strip : (head + 1) * 2 * strip] = query_ref[
                    half, :, pl.ds(start, strip), at : at + dim
                ].reshape(2 * strip, dim)
        own_id = spans_ref[2 * rank + half]

        def tiles(entries, keep):
            first = keep is not None
            held = [key_tile(slot) for slot, _ in entries]
            for one in range(sets):
                scores = [
                    lax.dot_general(
                        queries[one],
                        key,
                        (((1,), (1,)), ((), ())),
                        preferred_element_type=jnp.float32,
                    )
                    for key, _ in held
                ]
                if first:
                    scores[0] = jnp.where(keep, scores[0], -1e30)
                else:
                    old = tops[one]
                top = None if first else old
                for score, (_, away) in zip(scores, entries):
                    found = jnp.max(score, axis=1, keepdims=True) - away
                    found = jnp.broadcast_to(found, (stacked, dim))
                    top = found if top is None else jnp.maximum(top, found)
                total, mixed = None, None
                for score, (_, away), (_, value) in zip(scores, entries, held):
                    base = top + away
                    weight = [
                        jnp.exp2((score[:, part * dim : (part + 1) * dim] - base) * factor)
                        for part in range(parts)
                    ]
                    added = functools.reduce(jnp.add, weight)
                    weight = jnp.concatenate(weight, axis=1).astype(jnp.bfloat16)
                    product = jnp.dot(weight, value, preferred_element_type=jnp.float32)
                    total = added if total is None else total + added
                    mixed = product if mixed is None else mixed + product
                if not first:
                    scale = jnp.exp2((old - top) * factor)
                    total = totals[one] * scale + total
                    mixed = accums[one] * scale + mixed
                tops[one] = top
                totals[one] = total
                accums[one] = mixed

        def entry(slot):
            before = jnp.clip(own_id - spans_ref[slot], 0, 1)
            return slot, (1 - before).astype(jnp.float32) * 1e30

        shape = (group, 2, strip, span)
        token = (
            lax.broadcasted_iota(jnp.int32, shape, 1) * rows
            + lax.broadcasted_iota(jnp.int32, shape, 2)
            + start
        )
        keep = lax.broadcasted_iota(jnp.int32, shape, 3) <= token
        tiles([(2 * rank + half, 0.0), entry(2 * lax.rem(rank + 1 - half, ranks))], keep.reshape(stacked, span))

        def step(index, carry):
            block = lax.rem(rank + half * (1 + index) + (1 - half) * (2 + 2 * index), ranks)
            later = half + (1 - half) * 2 * lax.rem(rank + 3 + 2 * index, ranks)
            tiles([entry(2 * block), entry(half * 2 * block + later)], None)
            return carry

        lax.fori_loop(0, (ranks - 2 + ranks * half) // 2, step, 0)
        for one in range(sets):
            total = jnp.sum(totals[one], axis=1, keepdims=True)
            mixed = (accums[one] / total).astype(jnp.bfloat16)
            for head in range(group):
                at = (one * group + head) * dim
                heads_out[:, at : at + dim] = mixed[head * 2 * strip : (head + 1) * 2 * strip]

    def partial(index):
        found = jnp.dot(heads_out[...], weights[index], preferred_element_type=jnp.float32)
        return found.astype(jnp.bfloat16).reshape(2, strip, width)

    def add_pair(index):
        pair_copy(index).wait_recv()
        cross_out[index] = (
            cross_part[index, core].astype(jnp.float32) + pair_in[index].astype(jnp.float32)
        ).astype(jnp.bfloat16)
        cross_copy(index).start()

    def first(block, carry):
        attend_strip(1 - chip, block)

        @pl.when(block == 0)
        def _():
            for load in loads:
                load.wait()

        def one_chunk(chunk, inner):
            index = block * chunks + chunk
            cross_part[index] = partial(chunk)
            pair_copy(index).start()

            @pl.when(chunk > 0)
            def _():
                add_pair(index - 1)

            return inner

        lax.fori_loop(0, chunks, one_chunk, 0)
        add_pair(block * chunks + chunks - 1)
        return carry

    lax.fori_loop(0, strips, first, 0)

    def second(block, carry):
        attend_strip(chip, block)

        def one_chunk(chunk, inner):
            index = block * chunks + chunk
            own_part[index] = partial(chunk)
            own_copy(index).start()
            return inner

        lax.fori_loop(0, chunks, one_chunk, 0)
        return carry

    lax.fori_loop(0, strips, second, 0)

    for index in range(strips * chunks):
        own_copy(index).wait()
        pair_copy(index).wait_send()
        cross_copy(index).wait()
        total = own_part[index, core].astype(jnp.float32) + own_in[index].astype(jnp.float32)
        total = total + cross_in[index].astype(jnp.float32)
        block, chunk = index // chunks, index % chunks
        out_ref[block * strip : (block + 1) * strip, chunk * width : (chunk + 1) * width] = (
            total.astype(jnp.bfloat16)
        )


def combine(span_order, query, kv, w_out):
    depth, columns = w_out.shape
    rows = query.shape[2]
    ranks = span_order.shape[0]
    dim = kv.shape[1] // 2
    strip = rows // STRIPS
    width = columns // CHUNKS
    sets = 2
    stacked = depth // dim // sets * 2 * strip
    dma = pltpu.SemaphoreType.DMA
    bf16 = jnp.bfloat16
    steps = STRIPS * CHUNKS
    single = pltpu.VMEM((steps, strip, width), bf16)
    double = pltpu.VMEM((steps, 2, strip, width), bf16)
    state = pltpu.VMEM((sets, stacked, dim), jnp.float32)
    return pl.pallas_call(
        functools.partial(combine_kernel, ranks),
        out_shape=jax.ShapeDtypeStruct((rows, columns), bf16),
        in_specs=[pl.BlockSpec(memory_space=pltpu.SMEM)]
        + [pl.BlockSpec(memory_space=pltpu.VMEM)]
        + [pl.BlockSpec(memory_space=pl.ANY)] * 2,
        out_specs=pl.BlockSpec(memory_space=pltpu.VMEM),
        scratch_shapes=[
            pltpu.VMEM(kv.shape, bf16),
            pltpu.VMEM((CHUNKS, depth, width), bf16),
            pltpu.VMEM((sets, stacked, dim), bf16),
            state,
            state,
            state,
            pltpu.VMEM((2 * strip, depth), bf16),
            double,
            single,
            single,
            single,
            double,
            single,
            dma,
            dma((CHUNKS,)),
            dma((2, steps)),
            dma((2, steps)),
            dma((2, steps)),
        ],
        compiler_params=pltpu.CompilerParams(
            collective_id=1, has_side_effects=True, vmem_limit_bytes=60 * 2**20
        ),
        name="combine",
    )(span_order.reshape(-1), query, kv, w_out)


def body(tokens, w_query, key_matrix, value_matrix, w_out, span_order):
    rank = lax.axis_index("ctx")
    dim = key_matrix.shape[1]
    half = dim // 2
    rows = tokens.shape[0]
    span = 2 * rows
    mine = lax.dynamic_slice(span_order, (rank, jnp.int32(0)), (1, 2)).reshape(2)
    own_pos = (
        (mine[:, None] * span + jnp.arange(span, dtype=jnp.int32)[None, :])
        .reshape(-1)
        .astype(jnp.float32)
    )
    freq = ROPE_BASE ** (-(jnp.arange(half, dtype=jnp.float32) * 2.0) / dim)
    angle = own_pos[:, None] * freq[None, :]
    cosine, sine = jnp.cos(angle), jnp.sin(angle)
    cosine = jnp.concatenate([cosine, cosine], axis=1).reshape(2, 2, rows, dim)
    sine = jnp.concatenate([-sine, sine], axis=1).reshape(2, 2, rows, dim)
    query, kv = project(tokens, w_query, key_matrix, value_matrix, cosine, sine)
    return combine(span_order, query, kv.reshape(-1, 2 * dim), w_out)


def solution(mesh):
    return jax.shard_map(
        body,
        mesh=mesh,
        in_specs=(
            P(("ctx", "tp"), None),
            P(None, "tp"),
            P(None, "tp"),
            P(None, "tp"),
            P("tp", None),
            P(),
        ),
        out_specs=P(("ctx", "tp"), None),
        check_vma=False,
    )
```

```python
import functools
import math

import jax
import jax.numpy as jnp
from jax import lax
from jax.experimental import pallas as pl
from jax.experimental.pallas import tpu as pltpu
from jax.sharding import PartitionSpec as P

ROPE_BASE = 1000000.0


LOG2_E = 1.4426950408889634


MESH = pl.DeviceIdType.MESH
PIECES = 4
STRIPS = 4
CHUNKS = 4


def greet(devices):
    barrier = pltpu.get_barrier_semaphore()
    for device in devices:
        pl.semaphore_signal(barrier, inc=1, device_id=device, device_id_type=MESH)
    pl.semaphore_wait(barrier, len(devices))


def pair_places():
    place = lax.axis_index("tp")
    chip = place // 2
    core = place % 2
    return chip, core, {"tp": chip * 2 + 1 - core}, {"tp": (1 - chip) * 2 + core}


def project_kernel(
    columns_apart,
    ranks,
    tokens_ref,
    w_query_ref,
    key_matrix_ref,
    value_matrix_ref,
    cosine_ref,
    sine_ref,
    query_ref,
    kv_ref,
    weights,
    near,
    far,
    kv_near,
    kv_far,
    weight_sems,
    local_sems,
    near_sems,
    far_sems,
    swap_sems,
    column_sems,
    row_sems,
):
    chip, core, partner, across = pair_places()
    rank = lax.axis_index("ctx")
    tall = ranks // columns_apart
    wide = columns_apart
    row = rank // wide
    column = rank % wide
    count, piece = far.shape[0], far.shape[2]
    rows, width = tokens_ref.shape
    dim = key_matrix_ref.shape[1]
    blocks = weights.shape[0] - 1
    block = weights.shape[2]

    def along_rows(step):
        return {"ctx": lax.rem(row + step, tall) * wide + column}

    def along_columns(step):
        return {"ctx": row * wide + lax.rem(column + step, wide)}

    greet(
        [partner, across]
        + [along_rows(step) for step in range(1, tall)]
        + [along_columns(step) for step in range(1, wide)]
    )

    def remote(source, target, sems, index, device):
        return pltpu.make_async_remote_copy(
            src_ref=source,
            dst_ref=target,
            send_sem=sems.at[(0,) + index],
            recv_sem=sems.at[(1,) + index],
            device_id=device,
            device_id_type=MESH,
        )

    far_copies = []
    for part in range(count):
        copy = remote(
            tokens_ref.at[pl.ds(part * piece, piece)],
            far.at[part, core],
            far_sems,
            (part,),
            across,
        )
        far_copies.append(copy)
    far_copies[0].start()
    near_copy = remote(tokens_ref, near.at[core], near_sems, (), partner)
    near_copy.start()
    own_copy = pltpu.make_async_copy(tokens_ref, near.at[core], local_sems.at[0])
    own_copy.start()
    loads = [
        pltpu.make_async_copy(
            key_matrix_ref, weights.at[blocks, :, pl.ds(0, dim)], weight_sems.at[blocks]
        ),
        pltpu.make_async_copy(
            value_matrix_ref, weights.at[blocks, :, pl.ds(dim, dim)], weight_sems.at[blocks + 1]
        ),
    ]
    for index in range(blocks):
        loads.append(
            pltpu.make_async_copy(
                w_query_ref.at[:, pl.ds(index * block, block)],
                weights.at[index],
                weight_sems.at[index],
            )
        )
    for load in loads:
        load.start()

    def place(part, source):
        if part == 0:
            return kv_ref.at[source, chip]
        return kv_ref.at[source, 1 - chip, :, pl.ds((part - 1) * piece, piece)]

    def tables(part):
        if part == 0:
            return cosine_ref[chip], sine_ref[chip]
        span = slice((part - 1) * piece, part * piece)
        return cosine_ref[1 - chip, :, span], sine_ref[1 - chip, :, span]

    def flat(values):
        return values.reshape(values.shape[0] * values.shape[1], values.shape[2])

    def rotate(values, cosine, sine):
        return values * cosine + pltpu.roll(values, dim // 2, 1) * sine

    waits = []

    def share(part, staged):
        local = pltpu.make_async_copy(staged, place(part, rank), local_sems.at[1 + part])
        local.start()
        waits.append(local.wait)
        row_copies = []
        for step in range(1, tall):
            copy = remote(
                staged, place(part, rank), row_sems, (part, step - 1), along_rows(step)
            )
            copy.start()
            row_copies.append(copy)
            waits.append(copy.wait_send)
        for step in range(1, wide):
            copy = remote(
                staged, place(part, rank), column_sems, (part, 0, step - 1), along_columns(step)
            )
            copy.start()
            waits.append(copy.wait_send)

    def pass_on(part):
        for step in range(1, tall):
            source = lax.rem(row + tall - step, tall) * wide + column
            remote(
                place(part, source),
                place(part, source),
                row_sems,
                (part, step - 1),
                along_rows(step),
            ).wait_recv()
            for side in range(1, wide):
                copy = remote(
                    place(part, source),
                    place(part, source),
                    column_sems,
                    (part, step, side - 1),
                    along_columns(side),
                )
                copy.start()
                waits.append(copy.wait_send)

    def work(part, held, staged):
        cosine, sine = tables(part)
        cosine, sine = flat(cosine), flat(sine)
        both = jnp.dot(flat(held[...]), weights[blocks], preferred_element_type=jnp.float32)
        key = rotate(both[:, :dim], cosine, sine)
        kept = jnp.concatenate([key, both[:, dim:]], axis=1).astype(jnp.bfloat16)
        staged[...] = kept.reshape(staged.shape)
        share(part, staged)
        if part == 0:
            far_copies[1].start()
            for load in loads[2:]:
                load.wait()

        def one_block(index, carry):
            found = jnp.dot(flat(held[...]), weights[index], preferred_element_type=jnp.float32)
            for head in range(block // dim):
                turned = rotate(found[:, head * dim : (head + 1) * dim], cosine, sine)
                turned = turned.astype(jnp.bfloat16).reshape(2, -1, dim)
                lanes = pl.ds(pl.multiple_of(index * block + head * dim, dim), dim)
                if part == 0:
                    query_ref[chip, :, :, lanes] = turned
                else:
                    query_ref[1 - chip, :, (part - 1) * piece : part * piece, lanes] = turned
            return carry

        lax.fori_loop(0, blocks, one_block, 0)

    own_copy.wait()
    near_copy.wait()
    for load in loads[:2]:
        load.wait()
    work(0, near, kv_near)
    for part in range(count):
        far_copies[part].wait()
        if part + 2 < count:
            far_copies[part + 2].start()
        swap = remote(far.at[part, core], far.at[part, core], swap_sems, (part,), partner)
        swap.start()
        pass_on(part)
        swap.wait()
        work(part + 1, far.at[part], kv_far.at[part])
    pass_on(count)
    for part in range(count + 1):
        for step in range(tall):
            for side in range(1, wide):
                source = lax.rem(row + tall - step, tall) * wide + lax.rem(
                    column + wide - side, wide
                )
                remote(
                    place(part, source),
                    place(part, source),
                    column_sems,
                    (part, step, side - 1),
                    along_columns(side),
                ).wait_recv()
    for wait in waits:
        wait()


def project(tokens, w_query, key_matrix, value_matrix, cosine, sine):
    ranks = lax.axis_size("ctx")
    wide = 4 if ranks % 16 == 0 else 2
    rows, width = tokens.shape
    dim = key_matrix.shape[1]
    columns = w_query.shape[1]
    block = 2 * dim
    blocks = columns // block
    piece = rows // PIECES
    dma = pltpu.SemaphoreType.DMA
    bf16 = jnp.bfloat16
    return pl.pallas_call(
        functools.partial(project_kernel, wide, ranks),
        out_shape=(
            jax.ShapeDtypeStruct((2, 2, rows, columns), bf16),
            jax.ShapeDtypeStruct((ranks, 2, 2, rows, 2 * dim), bf16),
        ),
        in_specs=[pl.BlockSpec(memory_space=pl.ANY)] * 4
        + [pl.BlockSpec(memory_space=pltpu.VMEM)] * 2,
        out_specs=(pl.BlockSpec(memory_space=pltpu.VMEM), pl.BlockSpec(memory_space=pl.ANY)),
        scratch_shapes=[
            pltpu.VMEM((blocks + 1, width, block), bf16),
            pltpu.VMEM((2, rows, width), bf16),
            pltpu.VMEM((PIECES, 2, piece, width), bf16),
            pltpu.VMEM((2, rows, block), bf16),
            pltpu.VMEM((PIECES, 2, piece, block), bf16),
            dma((blocks + 2,)),
            dma((PIECES + 2,)),
            dma((2,)),
            dma((2, PIECES)),
            dma((2, PIECES)),
            dma((2, PIECES + 1, ranks // wide, wide - 1)),
            dma((2, PIECES + 1, ranks // wide - 1)),
        ],
        compiler_params=pltpu.CompilerParams(
            collective_id=0, has_side_effects=True, vmem_limit_bytes=60 * 2**20
        ),
        name="project",
    )(tokens, w_query, key_matrix, value_matrix, cosine, sine)


def combine_kernel(
    ranks,
    spans_ref,
    query_ref,
    kv_hbm_ref,
    w_ref,
    out_ref,
    kv_ref,
    weights,
    queries,
    tops,
    totals,
    accums,
    heads_out,
    cross_part,
    pair_in,
    cross_out,
    cross_in,
    own_part,
    own_in,
    kv_sem,
    weight_sems,
    pair_sems,
    cross_sems,
    own_sems,
):
    chip, core, partner, across = pair_places()
    rank = lax.axis_index("ctx")
    chunks, _, width = weights.shape
    rows = query_ref.shape[2]
    span = 2 * rows
    dim = kv_ref.shape[1] // 2
    strip = heads_out.shape[0] // 2
    strips = rows // strip
    sets, stacked, _ = queries.shape
    group = stacked // (2 * strip)
    parts = span // dim
    factor = LOG2_E / math.sqrt(dim)

    kv_load = pltpu.make_async_copy(kv_hbm_ref, kv_ref, kv_sem)
    kv_load.start()
    loads = [
        pltpu.make_async_copy(
            w_ref.at[:, pl.ds(index * width, width)], weights.at[index], weight_sems.at[index]
        )
        for index in range(chunks)
    ]
    greet([partner, across])
    kv_load.wait()
    for load in loads:
        load.start()

    def remote(source, target, sems, index, device):
        return pltpu.make_async_remote_copy(
            src_ref=source,
            dst_ref=target,
            send_sem=sems.at[0, index],
            recv_sem=sems.at[1, index],
            device_id=device,
            device_id_type=MESH,
        )

    def pair_copy(index):
        return remote(
            cross_part.at[index, 1 - core], pair_in.at[index], pair_sems, index, partner
        )

    def cross_copy(index):
        return remote(cross_out.at[index], cross_in.at[index], cross_sems, index, across)

    def own_copy(index):
        return remote(own_part.at[index, 1 - core], own_in.at[index], own_sems, index, partner)

    def key_tile(slot):
        start = pl.multiple_of(slot * span, span)
        return kv_ref[pl.ds(start, span), :dim], kv_ref[pl.ds(start, span), dim:]

    def attend_strip(half, index):
        start = pl.multiple_of(index * strip, strip)
        for one in range(sets):
            for head in range(group):
                at = (one * group + head) * dim
                queries[one, head * 2 * strip : (head + 1) * 2 * strip] = query_ref[
                    half, :, pl.ds(start, strip), at : at + dim
                ].reshape(2 * strip, dim)
        own_id = spans_ref[2 * rank + half]

        def tiles(entries, keep):
            first = keep is not None
            held = [key_tile(slot) for slot, _ in entries]
            for one in range(sets):
                scores = [
                    lax.dot_general(
                        queries[one],
                        key,
                        (((1,), (1,)), ((), ())),
                        preferred_element_type=jnp.float32,
                    )
                    for key, _ in held
                ]
                if first:
                    scores[0] = jnp.where(keep, scores[0], -1e30)
                else:
                    old = tops[one]
                top = None if first else old
                for score, (_, away) in zip(scores, entries):
                    found = jnp.max(score, axis=1, keepdims=True) - away
                    found = jnp.broadcast_to(found, (stacked, dim))
                    top = found if top is None else jnp.maximum(top, found)
                total, mixed = None, None
                for score, (_, away), (_, value) in zip(scores, entries, held):
                    base = top + away
                    weight = [
                        jnp.exp2((score[:, part * dim : (part + 1) * dim] - base) * factor)
                        for part in range(parts)
                    ]
                    added = functools.reduce(jnp.add, weight)
                    weight = jnp.concatenate(weight, axis=1).astype(jnp.bfloat16)
                    product = jnp.dot(weight, value, preferred_element_type=jnp.float32)
                    total = added if total is None else total + added
                    mixed = product if mixed is None else mixed + product
                if not first:
                    scale = jnp.exp2((old - top) * factor)
                    total = totals[one] * scale + total
                    mixed = accums[one] * scale + mixed
                tops[one] = top
                totals[one] = total
                accums[one] = mixed

        def entry(slot):
            before = jnp.clip(own_id - spans_ref[slot], 0, 1)
            return slot, (1 - before).astype(jnp.float32) * 1e30

        shape = (group, 2, strip, span)
        token = (
            lax.broadcasted_iota(jnp.int32, shape, 1) * rows
            + lax.broadcasted_iota(jnp.int32, shape, 2)
            + start
        )
        keep = lax.broadcasted_iota(jnp.int32, shape, 3) <= token
        def slot(index, at, side):
            apart = half * (2 * index + at // 2) + (1 - half) * (4 * index + at)
            return 2 * lax.rem(rank + apart, ranks) + half * side

        others = [entry(slot(0, at, side)) for at, side in ((1, 0), (2, 0), (3, 1))]
        tiles([(2 * rank + half, 0.0)] + others, keep.reshape(stacked, span))

        def step(index, carry):
            tiles([entry(slot(index, at, at % 2)) for at in range(4)], None)
            return carry

        lax.fori_loop(1, ranks * (1 + half) // 4, step, 0)
        for one in range(sets):
            total = jnp.sum(totals[one], axis=1, keepdims=True)
            mixed = (accums[one] / total).astype(jnp.bfloat16)
            for head in range(group):
                at = (one * group + head) * dim
                heads_out[:, at : at + dim] = mixed[head * 2 * strip : (head + 1) * 2 * strip]

    def partial(index):
        found = jnp.dot(heads_out[...], weights[index], preferred_element_type=jnp.float32)
        return found.astype(jnp.bfloat16).reshape(2, strip, width)

    def add_pair(index):
        pair_copy(index).wait_recv()
        cross_out[index] = (
            cross_part[index, core].astype(jnp.float32) + pair_in[index].astype(jnp.float32)
        ).astype(jnp.bfloat16)
        cross_copy(index).start()

    def first(block, carry):
        attend_strip(1 - chip, block)

        @pl.when(block == 0)
        def _():
            for load in loads:
                load.wait()

        def one_chunk(chunk, inner):
            index = block * chunks + chunk
            cross_part[index] = partial(chunk)
            pair_copy(index).start()

            @pl.when(chunk > 0)
            def _():
                add_pair(index - 1)

            return inner

        lax.fori_loop(0, chunks, one_chunk, 0)
        add_pair(block * chunks + chunks - 1)
        return carry

    lax.fori_loop(0, strips, first, 0)

    def second(block, carry):
        attend_strip(chip, block)

        def one_chunk(chunk, inner):
            index = block * chunks + chunk
            own_part[index] = partial(chunk)
            own_copy(index).start()
            return inner

        lax.fori_loop(0, chunks, one_chunk, 0)
        return carry

    lax.fori_loop(0, strips, second, 0)

    for index in range(strips * chunks):
        own_copy(index).wait()
        pair_copy(index).wait_send()
        cross_copy(index).wait()
        total = own_part[index, core].astype(jnp.float32) + own_in[index].astype(jnp.float32)
        total = total + cross_in[index].astype(jnp.float32)
        block, chunk = index // chunks, index % chunks
        out_ref[block * strip : (block + 1) * strip, chunk * width : (chunk + 1) * width] = (
            total.astype(jnp.bfloat16)
        )


def combine(span_order, query, kv, w_out):
    depth, columns = w_out.shape
    rows = query.shape[2]
    ranks = span_order.shape[0]
    dim = kv.shape[1] // 2
    strip = rows // STRIPS
    width = columns // CHUNKS
    sets = 2
    stacked = depth // dim // sets * 2 * strip
    dma = pltpu.SemaphoreType.DMA
    bf16 = jnp.bfloat16
    steps = STRIPS * CHUNKS
    single = pltpu.VMEM((steps, strip, width), bf16)
    double = pltpu.VMEM((steps, 2, strip, width), bf16)
    state = pltpu.VMEM((sets, stacked, dim), jnp.float32)
    return pl.pallas_call(
        functools.partial(combine_kernel, ranks),
        out_shape=jax.ShapeDtypeStruct((rows, columns), bf16),
        in_specs=[pl.BlockSpec(memory_space=pltpu.SMEM)]
        + [pl.BlockSpec(memory_space=pltpu.VMEM)]
        + [pl.BlockSpec(memory_space=pl.ANY)] * 2,
        out_specs=pl.BlockSpec(memory_space=pltpu.VMEM),
        scratch_shapes=[
            pltpu.VMEM(kv.shape, bf16),
            pltpu.VMEM((CHUNKS, depth, width), bf16),
            pltpu.VMEM((sets, stacked, dim), bf16),
            state,
            state,
            state,
            pltpu.VMEM((2 * strip, depth), bf16),
            double,
            single,
            single,
            single,
            double,
            single,
            dma,
            dma((CHUNKS,)),
            dma((2, steps)),
            dma((2, steps)),
            dma((2, steps)),
        ],
        compiler_params=pltpu.CompilerParams(
            collective_id=1, has_side_effects=True, vmem_limit_bytes=48 * 2**20
        ),
        name="combine",
    )(span_order.reshape(-1), query, kv, w_out)


def body(tokens, w_query, key_matrix, value_matrix, w_out, span_order):
    rank = lax.axis_index("ctx")
    dim = key_matrix.shape[1]
    half = dim // 2
    rows = tokens.shape[0]
    span = 2 * rows
    mine = lax.dynamic_slice(span_order, (rank, jnp.int32(0)), (1, 2)).reshape(2)
    own_pos = (
        (mine[:, None] * span + jnp.arange(span, dtype=jnp.int32)[None, :])
        .reshape(-1)
        .astype(jnp.float32)
    )
    freq = ROPE_BASE ** (-(jnp.arange(half, dtype=jnp.float32) * 2.0) / dim)
    angle = own_pos[:, None] * freq[None, :]
    cosine, sine = jnp.cos(angle), jnp.sin(angle)
    cosine = jnp.concatenate([cosine, cosine], axis=1).reshape(2, 2, rows, dim)
    sine = jnp.concatenate([-sine, sine], axis=1).reshape(2, 2, rows, dim)
    query, kv = project(tokens, w_query, key_matrix, value_matrix, cosine, sine)
    return combine(span_order, query, kv.reshape(-1, 2 * dim), w_out)


def solution(mesh):
    return jax.shard_map(
        body,
        mesh=mesh,
        in_specs=(
            P(("ctx", "tp"), None),
            P(None, "tp"),
            P(None, "tp"),
            P(None, "tp"),
            P("tp", None),
            P(),
        ),
        out_specs=P(("ctx", "tp"), None),
        check_vma=False,
    )
```

```python
import functools
import math

import jax
import jax.numpy as jnp
from jax import lax
from jax.experimental import pallas as pl
from jax.experimental.pallas import tpu as pltpu
from jax.sharding import PartitionSpec as P

ROPE_BASE = 1000000.0


LOG2_E = 1.4426950408889634


MESH = pl.DeviceIdType.MESH
PIECES = 4
STRIPS = 2
CHUNKS = 4


def greet(devices):
    barrier = pltpu.get_barrier_semaphore()
    for device in devices:
        pl.semaphore_signal(barrier, inc=1, device_id=device, device_id_type=MESH)
    pl.semaphore_wait(barrier, len(devices))


def pair_places():
    place = lax.axis_index("tp")
    chip = place // 2
    core = place % 2
    return chip, core, {"tp": chip * 2 + 1 - core}, {"tp": (1 - chip) * 2 + core}


def project_kernel(
    columns_apart,
    ranks,
    tokens_ref,
    w_query_ref,
    key_matrix_ref,
    value_matrix_ref,
    cosine_ref,
    sine_ref,
    query_ref,
    kv_ref,
    weights,
    near,
    far,
    kv_near,
    kv_far,
    weight_sems,
    local_sems,
    near_sems,
    far_sems,
    swap_sems,
    column_sems,
    row_sems,
):
    chip, core, partner, across = pair_places()
    rank = lax.axis_index("ctx")
    tall = ranks // columns_apart
    wide = columns_apart
    row = rank // wide
    column = rank % wide
    count, piece = far.shape[0], far.shape[2]
    rows, width = tokens_ref.shape
    dim = key_matrix_ref.shape[1]
    blocks = weights.shape[0] - 1
    block = weights.shape[2]

    def along_rows(step):
        return {"ctx": lax.rem(row + step, tall) * wide + column}

    def along_columns(step):
        return {"ctx": row * wide + lax.rem(column + step, wide)}

    greet(
        [partner, across]
        + [along_rows(step) for step in range(1, tall)]
        + [along_columns(step) for step in range(1, wide)]
    )

    def remote(source, target, sems, index, device):
        return pltpu.make_async_remote_copy(
            src_ref=source,
            dst_ref=target,
            send_sem=sems.at[(0,) + index],
            recv_sem=sems.at[(1,) + index],
            device_id=device,
            device_id_type=MESH,
        )

    far_copies = []
    for part in range(count):
        copy = remote(
            tokens_ref.at[pl.ds(part * piece, piece)],
            far.at[part, core],
            far_sems,
            (part,),
            across,
        )
        far_copies.append(copy)
    far_copies[0].start()
    near_copy = remote(tokens_ref, near.at[core], near_sems, (), partner)
    near_copy.start()
    own_copy = pltpu.make_async_copy(tokens_ref, near.at[core], local_sems.at[0])
    own_copy.start()
    loads = [
        pltpu.make_async_copy(
            key_matrix_ref, weights.at[blocks, :, pl.ds(0, dim)], weight_sems.at[blocks]
        ),
        pltpu.make_async_copy(
            value_matrix_ref, weights.at[blocks, :, pl.ds(dim, dim)], weight_sems.at[blocks + 1]
        ),
    ]
    for index in range(blocks):
        loads.append(
            pltpu.make_async_copy(
                w_query_ref.at[:, pl.ds(index * block, block)],
                weights.at[index],
                weight_sems.at[index],
            )
        )
    for load in loads:
        load.start()

    def place(part, source):
        if part == 0:
            return kv_ref.at[source, chip]
        return kv_ref.at[source, 1 - chip, :, pl.ds((part - 1) * piece, piece)]

    def tables(part):
        if part == 0:
            return flat(cosine_ref[chip]), flat(sine_ref[chip])
        span = slice((part - 1) * piece, part * piece)
        return flat(cosine_ref[1 - chip, :, span]), flat(sine_ref[1 - chip, :, span])

    def flat(values):
        return values.reshape(values.shape[0] * values.shape[1], values.shape[2])

    def rotate(values, cosine, sine):
        return values * cosine + pltpu.roll(values, dim // 2, 1) * sine

    waits = []

    def share(part, staged):
        local = pltpu.make_async_copy(staged, place(part, rank), local_sems.at[1 + part])
        local.start()
        waits.append(local.wait)
        row_copies = []
        for step in range(1, tall):
            copy = remote(
                staged, place(part, rank), row_sems, (part, step - 1), along_rows(step)
            )
            copy.start()
            row_copies.append(copy)
            waits.append(copy.wait_send)
        for step in range(1, wide):
            copy = remote(
                staged, place(part, rank), column_sems, (part, 0, step - 1), along_columns(step)
            )
            copy.start()
            waits.append(copy.wait_send)

    def pass_on(part):
        for step in range(1, tall):
            source = lax.rem(row + tall - step, tall) * wide + column
            remote(
                place(part, source),
                place(part, source),
                row_sems,
                (part, step - 1),
                along_rows(step),
            ).wait_recv()
            for side in range(1, wide):
                copy = remote(
                    place(part, source),
                    place(part, source),
                    column_sems,
                    (part, step, side - 1),
                    along_columns(side),
                )
                copy.start()
                waits.append(copy.wait_send)

    def work(part, held, staged):
        cosine, sine = tables(part)
        both = jnp.dot(flat(held[...]), weights[blocks], preferred_element_type=jnp.float32)
        key = rotate(both[:, :dim], cosine, sine)
        kept = jnp.concatenate([key, both[:, dim:]], axis=1).astype(jnp.bfloat16)
        staged[...] = kept.reshape(staged.shape)
        share(part, staged)

    def ask_near(index, carry):
        found = jnp.dot(flat(near[...]), weights[index], preferred_element_type=jnp.float32)
        cosine, sine = tables(0)
        for head in range(block // dim):
            turned = rotate(found[:, head * dim : (head + 1) * dim], cosine, sine)
            lanes = pl.ds(pl.multiple_of(index * block + head * dim, dim), dim)
            query_ref[chip, :, :, lanes] = turned.astype(jnp.bfloat16).reshape(2, rows, dim)
        return carry

    def ask_far(index, carry):
        held = far[...].reshape(count * 2 * piece, width)
        found = jnp.dot(held, weights[index], preferred_element_type=jnp.float32)
        for part in range(count):
            cosine, sine = tables(part + 1)
            for head in range(block // dim):
                one = found[2 * part * piece : 2 * (part + 1) * piece]
                turned = rotate(one[:, head * dim : (head + 1) * dim], cosine, sine)
                lanes = pl.ds(pl.multiple_of(index * block + head * dim, dim), dim)
                query_ref[1 - chip, :, part * piece : (part + 1) * piece, lanes] = turned.astype(
                    jnp.bfloat16
                ).reshape(2, piece, dim)
        return carry

    own_copy.wait()
    near_copy.wait()
    for load in loads[:2]:
        load.wait()
    work(0, near, kv_near)
    far_copies[1].start()
    for load in loads[2:]:
        load.wait()
    lax.fori_loop(0, blocks, ask_near, 0)
    for part in range(count):
        far_copies[part].wait()
        if part + 2 < count:
            far_copies[part + 2].start()
        swap = remote(far.at[part, core], far.at[part, core], swap_sems, (part,), partner)
        swap.start()
        pass_on(part)
        swap.wait()
        work(part + 1, far.at[part], kv_far.at[part])
    lax.fori_loop(0, blocks - 1, ask_far, 0)
    pass_on(count)
    ask_far(blocks - 1, 0)
    for part in range(count + 1):
        for step in range(tall):
            for side in range(1, wide):
                source = lax.rem(row + tall - step, tall) * wide + lax.rem(
                    column + wide - side, wide
                )
                remote(
                    place(part, source),
                    place(part, source),
                    column_sems,
                    (part, step, side - 1),
                    along_columns(side),
                ).wait_recv()
    for wait in waits:
        wait()


def project(tokens, w_query, key_matrix, value_matrix, cosine, sine):
    ranks = lax.axis_size("ctx")
    wide = 4 if ranks % 16 == 0 else 2
    rows, width = tokens.shape
    dim = key_matrix.shape[1]
    columns = w_query.shape[1]
    block = 2 * dim
    blocks = columns // block
    piece = rows // PIECES
    dma = pltpu.SemaphoreType.DMA
    bf16 = jnp.bfloat16
    return pl.pallas_call(
        functools.partial(project_kernel, wide, ranks),
        out_shape=(
            jax.ShapeDtypeStruct((2, 2, rows, columns), bf16),
            jax.ShapeDtypeStruct((ranks, 2, 2, rows, 2 * dim), bf16),
        ),
        in_specs=[pl.BlockSpec(memory_space=pl.ANY)] * 4
        + [pl.BlockSpec(memory_space=pltpu.VMEM)] * 2,
        out_specs=(pl.BlockSpec(memory_space=pltpu.VMEM), pl.BlockSpec(memory_space=pl.ANY)),
        scratch_shapes=[
            pltpu.VMEM((blocks + 1, width, block), bf16),
            pltpu.VMEM((2, rows, width), bf16),
            pltpu.VMEM((PIECES, 2, piece, width), bf16),
            pltpu.VMEM((2, rows, block), bf16),
            pltpu.VMEM((PIECES, 2, piece, block), bf16),
            dma((blocks + 2,)),
            dma((PIECES + 2,)),
            dma((2,)),
            dma((2, PIECES)),
            dma((2, PIECES)),
            dma((2, PIECES + 1, ranks // wide, wide - 1)),
            dma((2, PIECES + 1, ranks // wide - 1)),
        ],
        compiler_params=pltpu.CompilerParams(
            collective_id=0, has_side_effects=True, vmem_limit_bytes=60 * 2**20
        ),
        name="project",
    )(tokens, w_query, key_matrix, value_matrix, cosine, sine)


def combine_kernel(
    ranks,
    spans_ref,
    query_ref,
    kv_hbm_ref,
    w_ref,
    out_ref,
    kv_ref,
    weights,
    queries,
    tops,
    totals,
    accums,
    heads_out,
    cross_part,
    pair_in,
    cross_out,
    cross_in,
    own_part,
    own_in,
    kv_sem,
    weight_sems,
    pair_sems,
    cross_sems,
    own_sems,
):
    chip, core, partner, across = pair_places()
    rank = lax.axis_index("ctx")
    chunks, _, width = weights.shape
    rows = query_ref.shape[2]
    span = 2 * rows
    dim = kv_ref.shape[1] // 2
    strip = heads_out.shape[0] // 2
    strips = rows // strip
    sets, stacked, _ = queries.shape
    group = stacked // (2 * strip)
    parts = span // dim
    factor = LOG2_E / math.sqrt(dim)

    kv_load = pltpu.make_async_copy(kv_hbm_ref, kv_ref, kv_sem)
    kv_load.start()
    loads = [
        pltpu.make_async_copy(
            w_ref.at[:, pl.ds(index * width, width)], weights.at[index], weight_sems.at[index]
        )
        for index in range(chunks)
    ]
    greet([partner, across])
    kv_load.wait()
    for load in loads:
        load.start()

    def remote(source, target, sems, index, device):
        return pltpu.make_async_remote_copy(
            src_ref=source,
            dst_ref=target,
            send_sem=sems.at[0, index],
            recv_sem=sems.at[1, index],
            device_id=device,
            device_id_type=MESH,
        )

    def pair_copy(index):
        return remote(
            cross_part.at[index, 1 - core], pair_in.at[index], pair_sems, index, partner
        )

    def cross_copy(index):
        return remote(cross_out.at[index], cross_in.at[index], cross_sems, index, across)

    def own_copy(index):
        return remote(own_part.at[index, 1 - core], own_in.at[index], own_sems, index, partner)

    def key_tile(slot):
        start = pl.multiple_of(slot * span, span)
        return kv_ref[pl.ds(start, span), :dim], kv_ref[pl.ds(start, span), dim:]

    def attend_strip(half, index):
        start = pl.multiple_of(index * strip, strip)
        for one in range(sets):
            for head in range(group):
                at = (one * group + head) * dim
                queries[one, head * 2 * strip : (head + 1) * 2 * strip] = query_ref[
                    half, :, pl.ds(start, strip), at : at + dim
                ].reshape(2 * strip, dim)
        own_id = spans_ref[2 * rank + half]

        def tiles(entries, keep):
            first = keep is not None
            held = [key_tile(slot) for slot, _ in entries]
            for one in range(sets):
                scores = [
                    lax.dot_general(
                        queries[one],
                        key,
                        (((1,), (1,)), ((), ())),
                        preferred_element_type=jnp.float32,
                    )
                    for key, _ in held
                ]
                if first:
                    scores[0] = jnp.where(keep, scores[0], -1e30)
                else:
                    old = tops[one]
                top = None if first else old
                for score, (_, away) in zip(scores, entries):
                    found = jnp.max(score, axis=1, keepdims=True) - away
                    found = jnp.broadcast_to(found, (stacked, dim))
                    top = found if top is None else jnp.maximum(top, found)
                total, mixed = None, None
                for score, (_, away), (_, value) in zip(scores, entries, held):
                    base = top + away
                    weight = [
                        jnp.exp2((score[:, part * dim : (part + 1) * dim] - base) * factor)
                        for part in range(parts)
                    ]
                    added = functools.reduce(jnp.add, weight)
                    weight = jnp.concatenate(weight, axis=1).astype(jnp.bfloat16)
                    product = jnp.dot(weight, value, preferred_element_type=jnp.float32)
                    total = added if total is None else total + added
                    mixed = product if mixed is None else mixed + product
                if not first:
                    scale = jnp.exp2((old - top) * factor)
                    total = totals[one] * scale + total
                    mixed = accums[one] * scale + mixed
                tops[one] = top
                totals[one] = total
                accums[one] = mixed

        def entry(slot):
            before = jnp.clip(own_id - spans_ref[slot], 0, 1)
            return slot, (1 - before).astype(jnp.float32) * 1e30

        shape = (group, 2, strip, span)
        token = (
            lax.broadcasted_iota(jnp.int32, shape, 1) * rows
            + lax.broadcasted_iota(jnp.int32, shape, 2)
            + start
        )
        keep = lax.broadcasted_iota(jnp.int32, shape, 3) <= token
        def slot(index, at, side):
            apart = half * (2 * index + at // 2) + (1 - half) * (4 * index + at)
            return 2 * lax.rem(rank + apart, ranks) + half * side

        others = [entry(slot(0, at, side)) for at, side in ((1, 0), (2, 0), (3, 1))]
        tiles([(2 * rank + half, 0.0)] + others, keep.reshape(stacked, span))

        def step(index, carry):
            tiles([entry(slot(index, at, at % 2)) for at in range(4)], None)
            return carry

        lax.fori_loop(1, ranks * (1 + half) // 4, step, 0)
        for one in range(sets):
            total = jnp.sum(totals[one], axis=1, keepdims=True)
            mixed = (accums[one] / total).astype(jnp.bfloat16)
            for head in range(group):
                at = (one * group + head) * dim
                heads_out[:, at : at + dim] = mixed[head * 2 * strip : (head + 1) * 2 * strip]

    def partial(index):
        found = jnp.dot(heads_out[...], weights[index], preferred_element_type=jnp.float32)
        return found.astype(jnp.bfloat16).reshape(2, strip, width)

    def add_pair(index):
        pair_copy(index).wait_recv()
        cross_out[index] = (
            cross_part[index, core].astype(jnp.float32) + pair_in[index].astype(jnp.float32)
        ).astype(jnp.bfloat16)
        cross_copy(index).start()

    def first(block, carry):
        attend_strip(1 - chip, block)

        @pl.when(block == 0)
        def _():
            for load in loads:
                load.wait()

        def one_chunk(chunk, inner):
            index = block * chunks + chunk
            cross_part[index] = partial(chunk)
            pair_copy(index).start()

            @pl.when(chunk > 0)
            def _():
                add_pair(index - 1)

            return inner

        lax.fori_loop(0, chunks, one_chunk, 0)
        add_pair(block * chunks + chunks - 1)
        return carry

    lax.fori_loop(0, strips, first, 0)

    def second(block, carry):
        attend_strip(chip, block)

        def one_chunk(chunk, inner):
            index = block * chunks + chunk
            own_part[index] = partial(chunk)
            own_copy(index).start()
            return inner

        lax.fori_loop(0, chunks, one_chunk, 0)
        return carry

    lax.fori_loop(0, strips, second, 0)

    for index in range(strips * chunks):
        own_copy(index).wait()
        pair_copy(index).wait_send()
        cross_copy(index).wait()
        total = own_part[index, core].astype(jnp.float32) + own_in[index].astype(jnp.float32)
        total = total + cross_in[index].astype(jnp.float32)
        block, chunk = index // chunks, index % chunks
        out_ref[block * strip : (block + 1) * strip, chunk * width : (chunk + 1) * width] = (
            total.astype(jnp.bfloat16)
        )


def combine(span_order, query, kv, w_out):
    depth, columns = w_out.shape
    rows = query.shape[2]
    ranks = span_order.shape[0]
    dim = kv.shape[1] // 2
    strip = rows // STRIPS
    width = columns // CHUNKS
    sets = 3
    stacked = depth // dim // sets * 2 * strip
    dma = pltpu.SemaphoreType.DMA
    bf16 = jnp.bfloat16
    steps = STRIPS * CHUNKS
    single = pltpu.VMEM((steps, strip, width), bf16)
    double = pltpu.VMEM((steps, 2, strip, width), bf16)
    state = pltpu.VMEM((sets, stacked, dim), jnp.float32)
    return pl.pallas_call(
        functools.partial(combine_kernel, ranks),
        out_shape=jax.ShapeDtypeStruct((rows, columns), bf16),
        in_specs=[pl.BlockSpec(memory_space=pltpu.SMEM)]
        + [pl.BlockSpec(memory_space=pltpu.VMEM)]
        + [pl.BlockSpec(memory_space=pl.ANY)] * 2,
        out_specs=pl.BlockSpec(memory_space=pltpu.VMEM),
        scratch_shapes=[
            pltpu.VMEM(kv.shape, bf16),
            pltpu.VMEM((CHUNKS, depth, width), bf16),
            pltpu.VMEM((sets, stacked, dim), bf16),
            state,
            state,
            state,
            pltpu.VMEM((2 * strip, depth), bf16),
            double,
            single,
            single,
            single,
            double,
            single,
            dma,
            dma((CHUNKS,)),
            dma((2, steps)),
            dma((2, steps)),
            dma((2, steps)),
        ],
        compiler_params=pltpu.CompilerParams(
            collective_id=1, has_side_effects=True, vmem_limit_bytes=60 * 2**20
        ),
        name="combine",
    )(span_order.reshape(-1), query, kv, w_out)


def body(tokens, w_query, key_matrix, value_matrix, w_out, span_order):
    rank = lax.axis_index("ctx")
    dim = key_matrix.shape[1]
    half = dim // 2
    rows = tokens.shape[0]
    span = 2 * rows
    mine = lax.dynamic_slice(span_order, (rank, jnp.int32(0)), (1, 2)).reshape(2)
    own_pos = (
        (mine[:, None] * span + jnp.arange(span, dtype=jnp.int32)[None, :])
        .reshape(-1)
        .astype(jnp.float32)
    )
    freq = ROPE_BASE ** (-(jnp.arange(half, dtype=jnp.float32) * 2.0) / dim)
    angle = own_pos[:, None] * freq[None, :]
    cosine, sine = jnp.cos(angle), jnp.sin(angle)
    cosine = jnp.concatenate([cosine, cosine], axis=1).reshape(2, 2, rows, dim)
    sine = jnp.concatenate([-sine, sine], axis=1).reshape(2, 2, rows, dim)
    query, kv = project(tokens, w_query, key_matrix, value_matrix, cosine, sine)
    return combine(span_order, query, kv.reshape(-1, 2 * dim), w_out)


def solution(mesh):
    return jax.shard_map(
        body,
        mesh=mesh,
        in_specs=(
            P(("ctx", "tp"), None),
            P(None, "tp"),
            P(None, "tp"),
            P(None, "tp"),
            P("tp", None),
            P(),
        ),
        out_specs=P(("ctx", "tp"), None),
        check_vma=False,
    )
```

```python
import functools
import math

import jax
import jax.numpy as jnp
from jax import lax
from jax.experimental import pallas as pl
from jax.experimental.pallas import tpu as pltpu
from jax.sharding import PartitionSpec as P

ROPE_BASE = 1000000.0


LOG2_E = 1.4426950408889634


MESH = pl.DeviceIdType.MESH
PIECES = 8
STRIPS = 2
CHUNKS = 4


def greet(devices):
    barrier = pltpu.get_barrier_semaphore()
    for device in devices:
        pl.semaphore_signal(barrier, inc=1, device_id=device, device_id_type=MESH)
    pl.semaphore_wait(barrier, len(devices))


def pair_places():
    place = lax.axis_index("tp")
    chip = place // 2
    core = place % 2
    return chip, core, {"tp": chip * 2 + 1 - core}, {"tp": (1 - chip) * 2 + core}


def project_kernel(
    columns_apart,
    ranks,
    tokens_ref,
    w_query_ref,
    key_matrix_ref,
    value_matrix_ref,
    cosine_ref,
    sine_ref,
    query_ref,
    kv_ref,
    weights,
    near,
    far,
    kv_near,
    kv_far,
    weight_sems,
    local_sems,
    near_sems,
    far_sems,
    swap_sems,
    column_sems,
    row_sems,
):
    chip, core, partner, across = pair_places()
    rank = lax.axis_index("ctx")
    tall = ranks // columns_apart
    wide = columns_apart
    row = rank // wide
    column = rank % wide
    count, piece = far.shape[0], far.shape[2]
    rows, width = tokens_ref.shape
    dim = key_matrix_ref.shape[1]
    blocks = weights.shape[0] - 1
    block = weights.shape[2]

    def along_rows(step):
        return {"ctx": lax.rem(row + step, tall) * wide + column}

    def along_columns(step):
        return {"ctx": row * wide + lax.rem(column + step, wide)}

    greet(
        [partner, across]
        + [along_rows(step) for step in range(1, tall)]
        + [along_columns(step) for step in range(1, wide)]
    )

    def remote(source, target, sems, index, device):
        return pltpu.make_async_remote_copy(
            src_ref=source,
            dst_ref=target,
            send_sem=sems.at[(0,) + index],
            recv_sem=sems.at[(1,) + index],
            device_id=device,
            device_id_type=MESH,
        )

    far_copies = []
    for part in range(count):
        copy = remote(
            tokens_ref.at[pl.ds(part * piece, piece)],
            far.at[part, core],
            far_sems,
            (part,),
            across,
        )
        far_copies.append(copy)
    far_copies[0].start()
    far_copies[1].start()
    near_copy = remote(tokens_ref, near.at[core], near_sems, (), partner)
    near_copy.start()
    own_copy = pltpu.make_async_copy(tokens_ref, near.at[core], local_sems.at[0])
    own_copy.start()
    loads = [
        pltpu.make_async_copy(
            key_matrix_ref, weights.at[blocks, :, pl.ds(0, dim)], weight_sems.at[blocks]
        ),
        pltpu.make_async_copy(
            value_matrix_ref, weights.at[blocks, :, pl.ds(dim, dim)], weight_sems.at[blocks + 1]
        ),
    ]
    for index in range(blocks):
        loads.append(
            pltpu.make_async_copy(
                w_query_ref.at[:, pl.ds(index * block, block)],
                weights.at[index],
                weight_sems.at[index],
            )
        )
    for load in loads:
        load.start()

    def place(part, source):
        if part == 0:
            return kv_ref.at[source, chip]
        return kv_ref.at[source, 1 - chip, :, pl.ds((part - 1) * piece, piece)]

    def tables(part):
        if part == 0:
            return flat(cosine_ref[chip]), flat(sine_ref[chip])
        span = slice((part - 1) * piece, part * piece)
        return flat(cosine_ref[1 - chip, :, span]), flat(sine_ref[1 - chip, :, span])

    def flat(values):
        return values.reshape(values.shape[0] * values.shape[1], values.shape[2])

    def rotate(values, cosine, sine):
        return values * cosine + pltpu.roll(values, dim // 2, 1) * sine

    waits = []

    def share(part, staged):
        local = pltpu.make_async_copy(staged, place(part, rank), local_sems.at[1 + part])
        local.start()
        waits.append(local.wait)
        row_copies = []
        for step in range(1, tall):
            copy = remote(
                staged, place(part, rank), row_sems, (part, step - 1), along_rows(step)
            )
            copy.start()
            row_copies.append(copy)
            waits.append(copy.wait_send)
        for step in range(1, wide):
            copy = remote(
                staged, place(part, rank), column_sems, (part, 0, step - 1), along_columns(step)
            )
            copy.start()
            waits.append(copy.wait_send)

    def pass_on(part):
        for step in range(1, tall):
            source = lax.rem(row + tall - step, tall) * wide + column
            remote(
                place(part, source),
                place(part, source),
                row_sems,
                (part, step - 1),
                along_rows(step),
            ).wait_recv()
            for side in range(1, wide):
                copy = remote(
                    place(part, source),
                    place(part, source),
                    column_sems,
                    (part, step, side - 1),
                    along_columns(side),
                )
                copy.start()
                waits.append(copy.wait_send)

    def work(part, held, staged):
        cosine, sine = tables(part)
        both = jnp.dot(flat(held[...]), weights[blocks], preferred_element_type=jnp.float32)
        key = rotate(both[:, :dim], cosine, sine)
        kept = jnp.concatenate([key, both[:, dim:]], axis=1).astype(jnp.bfloat16)
        staged[...] = kept.reshape(staged.shape)
        share(part, staged)

    def ask_near(index, carry):
        found = jnp.dot(flat(near[...]), weights[index], preferred_element_type=jnp.float32)
        cosine, sine = tables(0)
        for head in range(block // dim):
            turned = rotate(found[:, head * dim : (head + 1) * dim], cosine, sine)
            lanes = pl.ds(pl.multiple_of(index * block + head * dim, dim), dim)
            query_ref[chip, :, :, lanes] = turned.astype(jnp.bfloat16).reshape(2, rows, dim)
        return carry

    def ask_far(index, carry):
        held = far[...].reshape(count * 2 * piece, width)
        found = jnp.dot(held, weights[index], preferred_element_type=jnp.float32)
        for part in range(count):
            cosine, sine = tables(part + 1)
            for head in range(block // dim):
                one = found[2 * part * piece : 2 * (part + 1) * piece]
                turned = rotate(one[:, head * dim : (head + 1) * dim], cosine, sine)
                lanes = pl.ds(pl.multiple_of(index * block + head * dim, dim), dim)
                query_ref[1 - chip, :, part * piece : (part + 1) * piece, lanes] = turned.astype(
                    jnp.bfloat16
                ).reshape(2, piece, dim)
        return carry

    own_copy.wait()
    near_copy.wait()
    for load in loads[:2]:
        load.wait()
    work(0, near, kv_near)
    far_copies[2].start()
    for load in loads[2:]:
        load.wait()
    lax.fori_loop(0, blocks, ask_near, 0)
    for part in range(count):
        far_copies[part].wait()
        if part + 3 < count:
            far_copies[part + 3].start()
        swap = remote(far.at[part, core], far.at[part, core], swap_sems, (part,), partner)
        swap.start()
        pass_on(part)
        swap.wait()
        work(part + 1, far.at[part], kv_far.at[part])
    ask_far(0, 0)
    pass_on(count)
    lax.fori_loop(1, blocks, ask_far, 0)
    for part in range(count + 1):
        for step in range(tall):
            for side in range(1, wide):
                source = lax.rem(row + tall - step, tall) * wide + lax.rem(
                    column + wide - side, wide
                )
                remote(
                    place(part, source),
                    place(part, source),
                    column_sems,
                    (part, step, side - 1),
                    along_columns(side),
                ).wait_recv()
    for wait in waits:
        wait()


def project(tokens, w_query, key_matrix, value_matrix, cosine, sine):
    ranks = lax.axis_size("ctx")
    wide = 4 if ranks % 16 == 0 else 2
    rows, width = tokens.shape
    dim = key_matrix.shape[1]
    columns = w_query.shape[1]
    block = 2 * dim
    blocks = columns // block
    piece = rows // PIECES
    dma = pltpu.SemaphoreType.DMA
    bf16 = jnp.bfloat16
    return pl.pallas_call(
        functools.partial(project_kernel, wide, ranks),
        out_shape=(
            jax.ShapeDtypeStruct((2, 2, rows, columns), bf16),
            jax.ShapeDtypeStruct((ranks, 2, 2, rows, 2 * dim), bf16),
        ),
        in_specs=[pl.BlockSpec(memory_space=pl.ANY)] * 4
        + [pl.BlockSpec(memory_space=pltpu.VMEM)] * 2,
        out_specs=(pl.BlockSpec(memory_space=pltpu.VMEM), pl.BlockSpec(memory_space=pl.ANY)),
        scratch_shapes=[
            pltpu.VMEM((blocks + 1, width, block), bf16),
            pltpu.VMEM((2, rows, width), bf16),
            pltpu.VMEM((PIECES, 2, piece, width), bf16),
            pltpu.VMEM((2, rows, block), bf16),
            pltpu.VMEM((PIECES, 2, piece, block), bf16),
            dma((blocks + 2,)),
            dma((PIECES + 2,)),
            dma((2,)),
            dma((2, PIECES)),
            dma((2, PIECES)),
            dma((2, PIECES + 1, ranks // wide, wide - 1)),
            dma((2, PIECES + 1, ranks // wide - 1)),
        ],
        compiler_params=pltpu.CompilerParams(
            collective_id=0, has_side_effects=True, vmem_limit_bytes=60 * 2**20
        ),
        name="project",
    )(tokens, w_query, key_matrix, value_matrix, cosine, sine)


def combine_kernel(
    ranks,
    spans_ref,
    query_ref,
    kv_hbm_ref,
    w_ref,
    out_ref,
    kv_ref,
    weights,
    queries,
    tops,
    totals,
    accums,
    heads_out,
    cross_part,
    pair_in,
    cross_out,
    cross_in,
    own_part,
    own_in,
    kv_sem,
    weight_sems,
    pair_sems,
    cross_sems,
    own_sems,
):
    chip, core, partner, across = pair_places()
    rank = lax.axis_index("ctx")
    chunks, _, width = weights.shape
    rows = query_ref.shape[2]
    span = 2 * rows
    dim = kv_ref.shape[1] // 2
    strip = heads_out.shape[0] // 2
    strips = rows // strip
    sets, stacked, _ = queries.shape
    group = stacked // (2 * strip)
    parts = span // dim
    factor = LOG2_E / math.sqrt(dim)

    kv_load = pltpu.make_async_copy(kv_hbm_ref, kv_ref, kv_sem)
    kv_load.start()
    loads = [
        pltpu.make_async_copy(
            w_ref.at[:, pl.ds(index * width, width)], weights.at[index], weight_sems.at[index]
        )
        for index in range(chunks)
    ]
    greet([partner, across])
    kv_load.wait()
    for load in loads:
        load.start()

    def remote(source, target, sems, index, device):
        return pltpu.make_async_remote_copy(
            src_ref=source,
            dst_ref=target,
            send_sem=sems.at[0, index],
            recv_sem=sems.at[1, index],
            device_id=device,
            device_id_type=MESH,
        )

    def pair_copy(index):
        return remote(
            cross_part.at[index, 1 - core], pair_in.at[index], pair_sems, index, partner
        )

    def cross_copy(index):
        return remote(cross_out.at[index], cross_in.at[index], cross_sems, index, across)

    def own_copy(index):
        return remote(own_part.at[index, 1 - core], own_in.at[index], own_sems, index, partner)

    def key_tile(slot):
        start = pl.multiple_of(slot * span, span)
        return kv_ref[pl.ds(start, span), :dim], kv_ref[pl.ds(start, span), dim:]

    def attend_strip(half, index):
        start = pl.multiple_of(index * strip, strip)
        for one in range(sets):
            for head in range(group):
                at = (one * group + head) * dim
                queries[one, head * 2 * strip : (head + 1) * 2 * strip] = query_ref[
                    half, :, pl.ds(start, strip), at : at + dim
                ].reshape(2 * strip, dim)
        own_id = spans_ref[2 * rank + half]

        def tiles(entries, keep):
            first = keep is not None
            held = [key_tile(slot) for slot, _ in entries]
            for one in range(sets):
                scores = [
                    lax.dot_general(
                        queries[one],
                        key,
                        (((1,), (1,)), ((), ())),
                        preferred_element_type=jnp.float32,
                    )
                    for key, _ in held
                ]
                if first:
                    scores[0] = jnp.where(keep, scores[0], -1e30)
                else:
                    old = tops[one]
                top = None if first else old
                for score, (_, away) in zip(scores, entries):
                    found = jnp.max(score, axis=1, keepdims=True) - away
                    found = jnp.broadcast_to(found, (stacked, dim))
                    top = found if top is None else jnp.maximum(top, found)
                total, mixed = None, None
                for score, (_, away), (_, value) in zip(scores, entries, held):
                    base = top + away
                    weight = [
                        jnp.exp2((score[:, part * dim : (part + 1) * dim] - base) * factor)
                        for part in range(parts)
                    ]
                    added = functools.reduce(jnp.add, weight)
                    weight = jnp.concatenate(weight, axis=1).astype(jnp.bfloat16)
                    product = jnp.dot(weight, value, preferred_element_type=jnp.float32)
                    total = added if total is None else total + added
                    mixed = product if mixed is None else mixed + product
                if not first:
                    scale = jnp.exp2((old - top) * factor)
                    total = totals[one] * scale + total
                    mixed = accums[one] * scale + mixed
                tops[one] = top
                totals[one] = total
                accums[one] = mixed

        def entry(slot):
            before = jnp.clip(own_id - spans_ref[slot], 0, 1)
            return slot, (1 - before).astype(jnp.float32) * 1e30

        shape = (group, 2, strip, span)
        token = (
            lax.broadcasted_iota(jnp.int32, shape, 1) * rows
            + lax.broadcasted_iota(jnp.int32, shape, 2)
            + start
        )
        keep = lax.broadcasted_iota(jnp.int32, shape, 3) <= token
        def slot(index, at, side):
            apart = half * (2 * index + at // 2) + (1 - half) * (4 * index + at)
            return 2 * lax.rem(rank + apart, ranks) + half * side

        others = [entry(slot(0, at, side)) for at, side in ((1, 0), (2, 0), (3, 1))]
        tiles([(2 * rank + half, 0.0)] + others, keep.reshape(stacked, span))

        def step(index, carry):
            tiles([entry(slot(index, at, at % 2)) for at in range(4)], None)
            return carry

        lax.fori_loop(1, ranks * (1 + half) // 4, step, 0)
        for one in range(sets):
            total = jnp.sum(totals[one], axis=1, keepdims=True)
            mixed = (accums[one] / total).astype(jnp.bfloat16)
            for head in range(group):
                at = (one * group + head) * dim
                heads_out[:, at : at + dim] = mixed[head * 2 * strip : (head + 1) * 2 * strip]

    def partial(index):
        found = jnp.dot(heads_out[...], weights[index], preferred_element_type=jnp.float32)
        return found.astype(jnp.bfloat16).reshape(2, strip, width)

    def add_pair(index):
        pair_copy(index).wait_recv()
        cross_out[index] = (
            cross_part[index, core].astype(jnp.float32) + pair_in[index].astype(jnp.float32)
        ).astype(jnp.bfloat16)
        cross_copy(index).start()

    def first(block, carry):
        attend_strip(1 - chip, block)

        @pl.when(block == 0)
        def _():
            for load in loads:
                load.wait()

        def one_chunk(chunk, inner):
            index = block * chunks + chunk
            cross_part[index] = partial(chunk)
            pair_copy(index).start()

            @pl.when(chunk > 0)
            def _():
                add_pair(index - 1)

            return inner

        lax.fori_loop(0, chunks, one_chunk, 0)
        add_pair(block * chunks + chunks - 1)
        return carry

    lax.fori_loop(0, strips, first, 0)

    def second(block, carry):
        attend_strip(chip, block)

        def one_chunk(chunk, inner):
            index = block * chunks + chunk
            own_part[index] = partial(chunk)
            own_copy(index).start()
            return inner

        lax.fori_loop(0, chunks, one_chunk, 0)
        return carry

    lax.fori_loop(0, strips, second, 0)

    for index in range(strips * chunks):
        own_copy(index).wait()
        pair_copy(index).wait_send()
        cross_copy(index).wait()
        total = own_part[index, core].astype(jnp.float32) + own_in[index].astype(jnp.float32)
        total = total + cross_in[index].astype(jnp.float32)
        block, chunk = index // chunks, index % chunks
        out_ref[block * strip : (block + 1) * strip, chunk * width : (chunk + 1) * width] = (
            total.astype(jnp.bfloat16)
        )


def combine(span_order, query, kv, w_out):
    depth, columns = w_out.shape
    rows = query.shape[2]
    ranks = span_order.shape[0]
    dim = kv.shape[1] // 2
    strip = rows // STRIPS
    width = columns // CHUNKS
    sets = 3
    stacked = depth // dim // sets * 2 * strip
    dma = pltpu.SemaphoreType.DMA
    bf16 = jnp.bfloat16
    steps = STRIPS * CHUNKS
    single = pltpu.VMEM((steps, strip, width), bf16)
    double = pltpu.VMEM((steps, 2, strip, width), bf16)
    state = pltpu.VMEM((sets, stacked, dim), jnp.float32)
    return pl.pallas_call(
        functools.partial(combine_kernel, ranks),
        out_shape=jax.ShapeDtypeStruct((rows, columns), bf16),
        in_specs=[pl.BlockSpec(memory_space=pltpu.SMEM)]
        + [pl.BlockSpec(memory_space=pltpu.VMEM)]
        + [pl.BlockSpec(memory_space=pl.ANY)] * 2,
        out_specs=pl.BlockSpec(memory_space=pltpu.VMEM),
        scratch_shapes=[
            pltpu.VMEM(kv.shape, bf16),
            pltpu.VMEM((CHUNKS, depth, width), bf16),
            pltpu.VMEM((sets, stacked, dim), bf16),
            state,
            state,
            state,
            pltpu.VMEM((2 * strip, depth), bf16),
            double,
            single,
            single,
            single,
            double,
            single,
            dma,
            dma((CHUNKS,)),
            dma((2, steps)),
            dma((2, steps)),
            dma((2, steps)),
        ],
        compiler_params=pltpu.CompilerParams(
            collective_id=1, has_side_effects=True, vmem_limit_bytes=60 * 2**20
        ),
        name="combine",
    )(span_order.reshape(-1), query, kv, w_out)


def body(tokens, w_query, key_matrix, value_matrix, w_out, span_order):
    rank = lax.axis_index("ctx")
    dim = key_matrix.shape[1]
    half = dim // 2
    rows = tokens.shape[0]
    span = 2 * rows
    mine = lax.dynamic_slice(span_order, (rank, jnp.int32(0)), (1, 2)).reshape(2)
    own_pos = (
        (mine[:, None] * span + jnp.arange(span, dtype=jnp.int32)[None, :])
        .reshape(-1)
        .astype(jnp.float32)
    )
    freq = ROPE_BASE ** (-(jnp.arange(half, dtype=jnp.float32) * 2.0) / dim)
    angle = own_pos[:, None] * freq[None, :]
    cosine, sine = jnp.cos(angle), jnp.sin(angle)
    cosine = jnp.concatenate([cosine, cosine], axis=1).reshape(2, 2, rows, dim)
    sine = jnp.concatenate([-sine, sine], axis=1).reshape(2, 2, rows, dim)
    query, kv = project(tokens, w_query, key_matrix, value_matrix, cosine, sine)
    return combine(span_order, query, kv.reshape(-1, 2 * dim), w_out)


def solution(mesh):
    return jax.shard_map(
        body,
        mesh=mesh,
        in_specs=(
            P(("ctx", "tp"), None),
            P(None, "tp"),
            P(None, "tp"),
            P(None, "tp"),
            P("tp", None),
            P(),
        ),
        out_specs=P(("ctx", "tp"), None),
        check_vma=False,
    )
```
